32 devices in a mesh: tile: 2 (over y), seg: 4 (over z), ord: 2 (over x), rep: 2 (over core).
Axes of the slice: x: 2, y: 2, z: 4, core: 2. Of those that a mesh axis runs over, the one named last changes fastest.
Arguments:
- points: bfloat16 [8192, 512], P(('tile', 'seg', 'ord')), parts along dimension 0, may hold values from -6 to 6
- counts: int32 [16], P(('tile', 'seg', 'ord')), parts along dimension 0, may hold values from 256 to 512, as said below
- neighbours: int32 [27, 8192], P(None, ('tile', 'seg', 'ord')), parts along dimension 1, may hold values from -1 to 767, as said below
- order_send: int32 [16, 512], P(('tile', 'seg', 'ord')), parts along dimension 0, may hold values from 0 to 511, as said below
- cpe_taps: bfloat16 [27, 512], replicated, may hold values from -1.25 to 1.25
- cpe_linear: bfloat16 [512, 512], P(None, 'rep'), may hold values from -0.25 to 0.25
- cpe_gain: float32 [512], replicated, may hold values from 0.5 to 1.5
- attn_gain: float32 [512], replicated, may hold values from 0.5 to 1.5
- qkv_weight: bfloat16 [512, 3, 512], P(None, None, 'rep')
- out_weight: bfloat16 [512, 512], P('rep'), may hold values from -0.25 to 0.25
- mlp_gain: float32 [512], replicated, may hold values from 0.5 to 1.5
- up_weight: bfloat16 [512, 2048], P(None, 'rep'), may hold values from -0.25 to 0.25
- down_weight: bfloat16 [2048, 512], P('rep'), may hold values from -0.125 to 0.125
Outputs:
- mixed: bfloat16 [8192, 512], P(('tile', 'seg', 'ord', 'rep')), parts along dimension 0
The draws below stay inside these ranges and needn't reach their ends.
There are 2 independent parts, one for each index of `tile`. The reference program is written for one: setup_inputs(seed, part) draws one part's arguments, and reference() takes and returns one part's arrays. A program takes and returns all parts, laid end to end along the dimension named above; an argument that names none is the same for every part. Nothing has to cross between parts.
Inputs may be any that keep to these rules, and one draw needn't show every extreme that they name: `counts`: some block has exactly 512 live points and some exactly 256. `neighbours`: rows of a block's window: 0 to 127 the previous block's last 128 live points, then the block's own 512 rows, then the next block's first 128 rows. Only live points are named, within 128 curve places of the point; -1 marks an empty slot; rows that are not live have -1 in every slot; tap 0 is the point itself. `order_send`: each row is a permutation of 0 to 511; entries b * 64 to (b + 1) * 64 - 1 are the local rows sent to patch b, and the first half of each such run lies below 256.
All inputs are finite; a program needn't handle non-finite values.
Results may differ from the reference program's by a relative error of at most 0.011.
The reference program's roundings to bfloat16 on the way count: a program that leaves them out, or rounds other values in their place, can miss the bound.
Values may be sent and summed in bfloat16 or wider, within the bound.
No kernel may reach another device: no remote copies, remote signals or barrier semaphores. Data moves between devices by JAX's collectives and lax.ppermute only.
A program may use at most 64 MiB of HBM per device.

```python
import jax
import jax.numpy as jnp
from jax import lax

D = 512
HEADS = 32
FF = 2048
PATCH = 512
TAPS = 27
RIM = 128
HEAD_DIM = 16
BLOCKS = 8
POINTS = 4096


def live_counts(key):
    first_key, second_key = jax.random.split(key)
    drawn = jax.random.randint(first_key, (BLOCKS,), PATCH // 2, PATCH + 1)
    chosen = jax.random.permutation(second_key, BLOCKS)
    return drawn.at[chosen[0]].set(PATCH).at[chosen[1]].set(PATCH // 2)


def draw_counts(key, part):
    shared = live_counts(key)
    return shared.astype(jnp.int32)


def draw_neighbours(key, part):
    live = live_counts(key)
    key = jax.random.fold_in(key, 7)
    offset_key, keep_key = jax.random.split(key)
    position = jnp.arange(PATCH, dtype=jnp.int32)[None, None, :]
    offsets = jax.random.randint(offset_key, (TAPS, BLOCKS, PATCH), -RIM, RIM + 1)
    keeping = jax.random.randint(keep_key, (TAPS, BLOCKS, PATCH), 0, 4) > 0
    live_here = live[None, :, None]
    last_live = position[0] == live[:, None] - 1
    offsets = offsets.at[0].set(0)
    offsets = offsets.at[1].set(jnp.where(last_live, RIM, offsets[1]))
    keeping = keeping.at[0].set(True)
    keeping = keeping.at[1].set(jnp.where(last_live, True, keeping[1]))
    target = position + offsets
    index = jnp.where(target < live_here, RIM + target, PATCH + RIM + target - live_here)
    usable = keeping & (position < live_here)
    index = jnp.where(usable, index, -1)
    return index.reshape(TAPS, BLOCKS * PATCH).astype(jnp.int32)


def draw_order_send(key, part):
    key = jax.random.fold_in(key, 11)
    per_peer = PATCH // BLOCKS
    half_rows = PATCH // 2
    block_keys = jax.random.split(key, BLOCKS)

    def one_block(block_key):
        first_key, second_key = jax.random.split(block_key)
        lower = jax.random.permutation(first_key, half_rows).reshape(BLOCKS, per_peer // 2)
        upper = half_rows + jax.random.permutation(second_key, half_rows).reshape(BLOCKS, per_peer // 2)
        return jnp.concatenate([lower, upper], axis=1).reshape(PATCH)
    return jax.vmap(one_block)(block_keys).astype(jnp.int32)


def draw_qkv_weight(key, part):
    key = jax.random.fold_in(key, 5)
    base_key = jax.random.fold_in(key, 0)
    base = jax.random.normal(base_key, (D, 3, D), jnp.float32) * D ** (-0.5)
    return base.astype(jnp.bfloat16)


def level_of(stream_key, dims, pieces, low, high):
    level = 1.0
    for dim, blocks in pieces:
        steps = jax.random.uniform(jax.random.fold_in(jax.random.fold_in(stream_key, 6), dim), (blocks,), jnp.float32, low / len(pieces), high / len(pieces))
        level = level * jnp.repeat(jnp.exp(steps), dims[dim] // blocks).reshape((-1,) + (1,) * (len(dims) - 1 - dim))
    return level


def normal_values(key, dims, width, limit, shards=(), held_as=jnp.bfloat16):
    level = level_of(key, dims, shards, -0.22, 0.18) if shards else 1.0
    values = jax.random.normal(key, dims, jnp.float32) * width * level
    return jnp.minimum(jnp.maximum(values, -limit), limit).astype(held_as)


def setup_inputs(seed: int = 0, part: int = 0) -> dict:
    keys = jax.random.split(jax.random.key(seed), 14)
    part_splits = jax.random.split(jax.random.fold_in(keys[13], part), 14)
    return {
        "points": normal_values(part_splits[0], (POINTS, D), 1.0, 6.0, ((0, 8),)),
        "counts": draw_counts(jax.random.fold_in(jax.random.fold_in(keys[13], part), 71), part),
        "neighbours": draw_neighbours(jax.random.fold_in(jax.random.fold_in(keys[13], part), 71), part),
        "order_send": draw_order_send(jax.random.fold_in(jax.random.fold_in(keys[13], part), 71), part),
        "cpe_taps": normal_values(keys[4], (TAPS, D), TAPS ** -0.5, 1.25),
        "cpe_linear": normal_values(keys[5], (D, D), D ** -0.5, 0.25, ((1, 2),)),
        "cpe_gain": jnp.clip(1.0 + 0.1 * jax.random.normal(keys[6], (D,), jnp.float32), 0.5, 1.5),
        "attn_gain": jnp.clip(1.0 + 0.1 * jax.random.normal(keys[7], (D,), jnp.float32), 0.5, 1.5),
        "qkv_weight": draw_qkv_weight(jax.random.fold_in(keys[13], 71), part),
        "out_weight": normal_values(keys[9], (D, D), D ** -0.5, 0.25, ((0, 2),)),
        "mlp_gain": jnp.clip(1.0 + 0.1 * jax.random.normal(keys[10], (D,), jnp.float32), 0.5, 1.5),
        "up_weight": normal_values(keys[11], (D, FF), D ** -0.5, 0.25, ((1, 2),)),
        "down_weight": normal_values(keys[12], (FF, D), FF ** -0.5, 0.125, ((0, 2),)),
    }


epsilon = 1e-06
masked_score = -1e+30

def normalize(values, gain):
    centred = values - lax.optimization_barrier(jnp.mean(values, axis=-1, keepdims=True))
    spread = lax.optimization_barrier(jnp.mean(centred * centred, axis=-1, keepdims=True))
    return centred * lax.rsqrt(spread + epsilon) * gain.astype(jnp.float32)

def edge_rows(block, live_count):
    tail_start = (live_count - RIM).astype(jnp.int32)
    return (block[:RIM], lax.dynamic_slice_in_dim(block, tail_start, RIM, 0))

def pick_rows(window, index):
    return jnp.take(window, index, axis=0)

def reference(points, counts, neighbours, order_send, cpe_taps, cpe_linear, cpe_gain, attn_gain, qkv_weight, out_weight, mlp_gain, up_weight, down_weight):
    blocks = points.reshape(BLOCKS, PATCH, D)
    head_edges, tail_edges = jax.vmap(edge_rows)(blocks, counts)
    empty = jnp.zeros((1, RIM, D), points.dtype)
    before = jnp.concatenate([empty, tail_edges[:-1]], axis=0)
    after = jnp.concatenate([head_edges[1:], empty], axis=0)
    windows = jnp.concatenate([before, blocks, after], axis=1)
    links = neighbours.reshape(TAPS, BLOCKS, PATCH)
    tap_weights = cpe_taps.astype(jnp.float32)
    convolved = jnp.zeros((BLOCKS, PATCH, D), jnp.float32)
    for tap_index in range(TAPS):
        index = links[tap_index]
        picked = jax.vmap(pick_rows)(windows, jnp.maximum(index, 0).astype(jnp.int32)).astype(jnp.float32)
        convolved = convolved + jnp.where((index >= 0)[:, :, None], picked * tap_weights[tap_index], 0.0)
    encoded = jnp.dot(convolved.reshape(POINTS, D).astype(jnp.bfloat16), cpe_linear, preferred_element_type=jnp.float32).astype(jnp.bfloat16)
    stream = points.astype(jnp.float32) + normalize(encoded.astype(jnp.float32), cpe_gain)
    normed = normalize(stream, attn_gain).astype(jnp.bfloat16)
    live_mask = (jnp.arange(PATCH, dtype=jnp.int32)[None, :] < counts[:, None]).reshape(POINTS)
    per_peer = PATCH // BLOCKS
    sources = order_send.reshape(BLOCKS, BLOCKS, per_peer) + (jnp.arange(BLOCKS, dtype=jnp.int32) * PATCH)[:, None, None]
    members = sources.transpose(1, 0, 2).reshape(BLOCKS, PATCH).astype(jnp.int32)
    score_scale = HEAD_DIM ** (-0.5)
    qkv_full = qkv_weight.astype(jnp.float32)

    def attend_patch(member_rows):
        feats = jnp.take(normed, member_rows, axis=0).astype(jnp.float32)
        live_keys = jnp.take(live_mask, member_rows, axis=0)
        projected = lax.optimization_barrier(jnp.einsum('rc,ctj->trj', feats, qkv_full).astype(jnp.bfloat16)).astype(jnp.float32)
        split_heads = projected.reshape(3, PATCH, HEADS, HEAD_DIM)
        scores = jnp.einsum('qhd,khd->hqk', split_heads[0], split_heads[1]) * score_scale
        scores = jnp.where(live_keys[None, None, :], scores, masked_score)
        row_max = lax.optimization_barrier(jnp.max(scores, axis=2, keepdims=True))
        exponent = jnp.exp(scores - row_max)
        weights = lax.optimization_barrier((exponent / lax.optimization_barrier(jnp.sum(exponent, axis=2, keepdims=True))).astype(jnp.bfloat16)).astype(jnp.float32)
        attended = jnp.einsum('hqk,khd->qhd', weights, split_heads[2]).astype(jnp.bfloat16)
        return attended.reshape(PATCH, D)
    attended = lax.map(attend_patch, members)
    restored = jnp.zeros((POINTS, D), jnp.bfloat16).at[members.reshape(POINTS)].set(attended.reshape(POINTS, D))
    mid_stream = stream + jnp.dot(restored, out_weight, preferred_element_type=jnp.float32)
    mlp_in = normalize(mid_stream, mlp_gain).astype(jnp.bfloat16)
    hidden = jax.nn.gelu(jnp.dot(mlp_in, up_weight, preferred_element_type=jnp.float32), approximate=True).astype(jnp.bfloat16)
    mixed = mid_stream + jnp.dot(hidden, down_weight, preferred_element_type=jnp.float32)
    return jnp.where(live_mask[:, None], mixed, 0.0).astype(jnp.bfloat16)
```

```python
import jax
import jax.numpy as jnp
from jax import lax
from jax.experimental import pallas as pl
from jax.experimental.pallas import tpu as pltpu
from jax.sharding import PartitionSpec as P

RIM = 128
HEAD_DIM = 16
LANES = 128
EPSILON = 1e-06
MASKED = -1e30
DEAD_MARK = 16384.0
DEAD_LEVEL = 8192.0

VMEM = pl.BlockSpec(memory_space=pltpu.VMEM)
SMEM = pl.BlockSpec(memory_space=pltpu.SMEM)
HBM = pl.BlockSpec(memory_space=pltpu.HBM)
MIB = 1 << 20


def dot(a, b):
    return jnp.dot(a, b, preferred_element_type=jnp.float32)


def dot_first(a, b):
    return lax.dot_general(a, b, (((0,), (0,)), ((), ())), preferred_element_type=jnp.float32)


def dot_last(a, b):
    return lax.dot_general(a, b, (((1,), (1,)), ((), ())), preferred_element_type=jnp.float32)


def normalize(values, gain):
    centred = values - jnp.mean(values, axis=-1, keepdims=True)
    spread = jnp.mean(centred * centred, axis=-1, keepdims=True)
    return centred * lax.rsqrt(spread + EPSILON) * gain


def gelu(x):
    return 0.5 * x * (1.0 + jnp.tanh((2.0 / jnp.pi) ** 0.5 * (x + 0.044715 * (x * x * x))))


def encode_kernel(
    live_ref, before_ref, points_ref, after_ref, neighbours_ref, order_ref, taps_ref,
    linear_own_ref, linear_other_ref, cpe_gain_ref, attn_gain_ref,
    stream_ref, send_ref,
    padded, window, acc, encoded,
):
    rows, half = points_ref.shape[0], stream_ref.shape[0]
    taps = taps_ref.shape[0]
    span = half + 2 * RIM
    rep = live_ref[1]
    live = live_ref[0]
    base = pl.multiple_of(rep * half, half)
    padded[:RIM] = before_ref[...]
    padded[RIM : RIM + rows] = points_ref[...]
    padded[RIM + rows :] = jnp.zeros_like(padded[RIM + rows :])
    place = lax.broadcasted_iota(jnp.int32, (span, RIM), 0) + (base - RIM - live)
    hot = (place == lax.broadcasted_iota(jnp.int32, (span, RIM), 1)).astype(jnp.bfloat16)
    shifted = dot(hot, after_ref[...])
    place = lax.broadcasted_iota(jnp.int32, (span, points_ref.shape[1]), 0) + (base - RIM - live)
    window[...] = jnp.where(
        place >= 0, shifted, padded[pl.ds(base, span)].astype(jnp.float32)
    ).astype(jnp.bfloat16)

    index = neighbours_ref[:, pl.ds(base, half)]
    index = jnp.where(index >= RIM + rows, index - rows + live, index) - base
    index = index.T
    spots = lax.broadcasted_iota(jnp.int32, (half, span), 1)
    for tap in range(taps):
        hot = (spots == index[:, tap : tap + 1]).astype(jnp.bfloat16)
        term = dot(hot, window[...]) * taps_ref[tap : tap + 1, :].astype(jnp.float32)
        if tap == 0:
            acc[...] = term
        else:
            acc[...] += term
    convolved = acc[...].astype(jnp.bfloat16)
    columns = linear_own_ref.shape[1]
    own_at = pl.multiple_of(rep * columns, columns)
    other_at = pl.multiple_of((1 - rep) * columns, columns)
    encoded[:, pl.ds(own_at, columns)] = dot(convolved, linear_own_ref[...])
    encoded[:, pl.ds(other_at, columns)] = dot(convolved, linear_other_ref[...])
    rounded = encoded[...].astype(jnp.bfloat16).astype(jnp.float32)
    own_points = points_ref[pl.ds(base, half)].astype(jnp.float32)
    stream = own_points + normalize(rounded, cpe_gain_ref[...])
    stream_ref[...] = stream
    normed = normalize(stream, attn_gain_ref[...])
    row = lax.broadcasted_iota(jnp.int32, normed.shape, 0) + base
    marked = jnp.where(row < live, normed, DEAD_MARK).astype(jnp.bfloat16)
    source = lax.broadcasted_iota(jnp.int32, (half, half), 0) + base
    hot = (source == order_ref[...]).astype(jnp.bfloat16)
    send_ref[...] = dot_first(hot, marked).astype(jnp.bfloat16)


def start_copies(sources, targets, semaphores):
    copies = [
        pltpu.make_async_copy(source, target, semaphores.at[at])
        for at, (source, target) in enumerate(zip(sources, targets))
    ]
    for copy in copies:
        copy.start()
    return copies


def attend_kernel(
    own_ref, other_ref, weight_own_hbm, weight_other_hbm, out_ref,
    feats, dead_block, weight_own_ref, weight_other_ref, semaphores,
):
    copies = start_copies(
        (weight_own_hbm, weight_other_hbm), (weight_own_ref, weight_other_ref), semaphores
    )
    half = own_ref.shape[0]
    group_heads = LANES // HEAD_DIM
    lane = lax.broadcasted_iota(jnp.int32, (2 * half, LANES), 1)
    for at, ref in ((0, own_ref), (half, other_ref)):
        rows = ref[...].astype(jnp.float32)
        dead = rows > DEAD_LEVEL
        feats[at : at + half] = jnp.where(dead, 0.0, rows).astype(jnp.bfloat16)
        dead_block[at : at + half] = jnp.where(
            dead[:, :LANES] & (lane[:half] == 0), MASKED, 0.0
        ).astype(jnp.bfloat16)
    first = (lane[:half] == 0).astype(jnp.bfloat16)
    for side, weight_ref in enumerate((weight_own_ref, weight_other_ref)):
        columns = weight_ref.shape[2]
        copies[side].wait()
        queries = dot(feats[:half], weight_ref[0]).astype(jnp.bfloat16) * (HEAD_DIM ** -0.5)
        queries = queries.astype(jnp.bfloat16)
        keys = dot(feats[...], weight_ref[1]).astype(jnp.bfloat16)
        values = dot(feats[...], weight_ref[2]).astype(jnp.bfloat16)
        for group in range(columns // LANES):
            span = slice(group * LANES, (group + 1) * LANES)
            query = jnp.concatenate([queries[:, span], first], axis=1)
            total = None
            for head in range(group_heads):
                mine = lane // HEAD_DIM == head
                key = jnp.concatenate(
                    [jnp.where(mine, keys[:, span], 0.0).astype(jnp.bfloat16), dead_block[...]], axis=1
                )
                value = jnp.concatenate(
                    [
                        jnp.where(mine, values[:, span], 0.0).astype(jnp.bfloat16),
                        mine.astype(jnp.bfloat16),
                    ],
                    axis=1,
                )
                scores = dot_last(query, key)
                exponent = jnp.exp(scores - jnp.max(scores, axis=1, keepdims=True))
                term = dot(exponent.astype(jnp.bfloat16), value)
                total = term if total is None else total + term
            out_ref[:, side * columns + group * LANES : side * columns + (group + 1) * LANES] = (
                total[:, :LANES] / total[:, LANES:]
            ).astype(jnp.bfloat16)


def mix_kernel(
    live_ref, returned_ref, order_ref, stream_ref, gain_ref, *refs,
):
    weights, mixed_ref = refs[:6], refs[6]
    out_own_ref, out_other_ref, up_own_ref, up_other_ref, down_ref, semaphores, hidden = refs[7:]
    size = up_own_ref.shape[1]
    copies = start_copies(
        weights,
        (
            out_own_ref, out_other_ref, up_own_ref, up_other_ref,
            down_ref.at[:size], down_ref.at[size:],
        ),
        semaphores,
    )
    half = returned_ref.shape[0]
    columns = out_own_ref.shape[0]
    live = live_ref[0]
    base = live_ref[1] * half
    row = lax.broadcasted_iota(jnp.int32, (half, half), 0) + base
    hot = (row == order_ref[...]).astype(jnp.bfloat16)
    restored = dot(hot, returned_ref[...]).astype(jnp.bfloat16)
    copies[0].wait()
    copies[1].wait()
    mid = (
        stream_ref[...]
        + dot(restored[:, :columns], out_own_ref[...])
        + dot(restored[:, columns:], out_other_ref[...])
    )
    mlp_in = normalize(mid, gain_ref[...]).astype(jnp.bfloat16)
    chunk = min(size, 512)
    for side, up_ref in enumerate((up_own_ref, up_other_ref)):
        copies[2 + side].wait()
        for at in range(0, size, chunk):
            lifted = dot(mlp_in, up_ref[:, at : at + chunk])
            hidden[:, side * size + at : side * size + at + chunk] = gelu(lifted).astype(jnp.bfloat16)
    copies[4].wait()
    copies[5].wait()
    mixed = mid + dot(hidden[...], down_ref[...])
    row = lax.broadcasted_iota(jnp.int32, mixed.shape, 0) + base
    mixed_ref[...] = jnp.where(row < live, mixed, 0.0).astype(jnp.bfloat16)


def call(kernel, out_shape, ins, scratch, flops, transcendentals, limit):
    bytes_accessed = 4 * MIB
    return pl.pallas_call(
        kernel,
        out_shape=out_shape,
        in_specs=ins,
        out_specs=jax.tree.map(lambda _: VMEM, out_shape),
        scratch_shapes=scratch,
        compiler_params=pltpu.CompilerParams(vmem_limit_bytes=limit),
        cost_estimate=pl.CostEstimate(
            flops=flops, bytes_accessed=bytes_accessed, transcendentals=transcendentals
        ),
    )


def shards(
    points,
    counts,
    neighbours,
    order_send,
    cpe_taps,
    cpe_linear,
    cpe_gain,
    attn_gain,
    qkv_weight,
    out_weight,
    mlp_gain,
    up_weight,
    down_weight,
):
    rows, width = points.shape
    half = rows // 2
    taps = neighbours.shape[0]
    ring = ("seg", "ord")
    peers = lax.axis_size("seg") * lax.axis_size("ord")
    per_peer = rows // peers
    per_half = per_peer // 2
    rep = lax.axis_index("rep")
    live = counts[0]
    scalars = jnp.stack([live, rep.astype(jnp.int32)])

    def swap(array):
        return lax.ppermute(array, "rep", [(0, 1), (1, 0)])

    up_hop = [(i, i + 1) for i in range(peers - 1)]
    down_hop = [(i + 1, i) for i in range(peers - 1)]
    after = lax.ppermute(points[:RIM], ring, down_hop)
    before = lax.ppermute(lax.dynamic_slice_in_dim(points, live - RIM, RIM, 0), ring, up_hop)
    linear_other = swap(cpe_linear)
    qkv_own = qkv_weight.transpose(1, 0, 2)
    qkv_other = swap(qkv_own)
    out_other = swap(out_weight)
    up_other = swap(up_weight)
    down_other = swap(down_weight)
    order = lax.dynamic_index_in_dim(
        order_send.reshape(peers, 2, per_half), rep, 1, keepdims=False
    ).reshape(1, half)

    span = half + 2 * RIM
    stream, send = call(
        encode_kernel,
        [
            jax.ShapeDtypeStruct((half, width), jnp.float32),
            jax.ShapeDtypeStruct((half, width), jnp.bfloat16),
        ],
        [SMEM] + [VMEM] * 10,
        [
            pltpu.VMEM((rows + 2 * RIM, width), jnp.bfloat16),
            pltpu.VMEM((span, width), jnp.bfloat16),
            pltpu.VMEM((half, width), jnp.float32),
            pltpu.VMEM((half, width), jnp.float32),
        ],
        2 * taps * half * span * width,
        half * 4,
        24 * MIB,
    )(
        scalars, before, points, after, neighbours, order, cpe_taps, cpe_linear, linear_other,
        cpe_gain.reshape(1, width), attn_gain.reshape(1, width),
    )

    arrived = lax.all_to_all(
        send.reshape(peers, per_half, width), ring, split_axis=0, concat_axis=0, tiled=True
    ).reshape(half, width)
    arrived_other = swap(arrived)
    attended = call(
        attend_kernel,
        jax.ShapeDtypeStruct((half, width), jnp.bfloat16),
        [VMEM] * 2 + [HBM] * 2,
        [pltpu.VMEM((rows, width), jnp.bfloat16), pltpu.VMEM((rows, LANES), jnp.bfloat16)]
        + [pltpu.VMEM(qkv_own.shape, jnp.bfloat16)] * 2
        + [pltpu.SemaphoreType.DMA((2,))],
        2 * (width // HEAD_DIM) * half * rows * 512,
        (width // HEAD_DIM) * half * rows,
        24 * MIB,
    )(arrived, arrived_other, qkv_own, qkv_other)
    returned = lax.all_to_all(
        attended.reshape(peers, per_half, width), ring, split_axis=0, concat_axis=0, tiled=True
    ).reshape(half, width)
    hidden = 2 * up_weight.shape[1]
    weights = (out_weight, out_other, up_weight, up_other, down_weight, down_other)
    return call(
        mix_kernel,
        jax.ShapeDtypeStruct((half, width), jnp.bfloat16),
        [SMEM] + [VMEM] * 4 + [HBM] * 6,
        [pltpu.VMEM(weight.shape, weight.dtype) for weight in weights[:4]]
        + [
            pltpu.VMEM((hidden, width), down_weight.dtype),
            pltpu.SemaphoreType.DMA((6,)),
            pltpu.VMEM((half, hidden), jnp.bfloat16),
        ],
        2 * half * width * (width + half + 2 * hidden),
        half * hidden,
        32 * MIB,
    )(
        scalars, returned, order, stream, mlp_gain.reshape(1, width), *weights
    )


def solution(mesh):
    placed = (
        P(("tile", "seg", "ord"), None),
        P(("tile", "seg", "ord")),
        P(None, ("tile", "seg", "ord")),
        P(("tile", "seg", "ord"), None),
        P(),
        P(None, "rep"),
        P(),
        P(),
        P(None, None, "rep"),
        P("rep", None),
        P(),
        P(None, "rep"),
        P("rep", None),
    )
    return jax.shard_map(
        shards,
        mesh=mesh,
        in_specs=placed,
        out_specs=P(("tile", "seg", "ord", "rep"), None),
        check_vma=False,
    )
```

```python
import functools

import jax
import jax.numpy as jnp
from jax import lax
from jax.experimental import pallas as pl
from jax.experimental.pallas import tpu as pltpu
from jax.sharding import PartitionSpec as P

RIM = 128
HEAD_DIM = 16
LANES = 128
EPSILON = 1e-06
MASKED = -1e30
DEAD_MARK = 16384.0
DEAD_LEVEL = 8192.0

VMEM = pl.BlockSpec(memory_space=pltpu.VMEM)
SMEM = pl.BlockSpec(memory_space=pltpu.SMEM)
HBM = pl.BlockSpec(memory_space=pltpu.HBM)
MIB = 1 << 20


def dot(a, b):
    return jnp.dot(a, b, preferred_element_type=jnp.float32)


def dot_first(a, b):
    return lax.dot_general(a, b, (((0,), (0,)), ((), ())), preferred_element_type=jnp.float32)


def dot_last(a, b):
    return lax.dot_general(a, b, (((1,), (1,)), ((), ())), preferred_element_type=jnp.float32)


def normalize(values, gain):
    centred = values - jnp.mean(values, axis=-1, keepdims=True)
    spread = jnp.mean(centred * centred, axis=-1, keepdims=True)
    return centred * lax.rsqrt(spread + EPSILON) * gain


def gelu(x):
    return 0.5 * x * (1.0 + jnp.tanh((2.0 / jnp.pi) ** 0.5 * (x + 0.044715 * (x * x * x))))


def own_order(order_ref, base, rep, half, per_half):
    slots = order_ref.shape[1]
    local = jnp.clip(order_ref[...] - base, 0, half - 1).astype(jnp.float32)
    local = jnp.broadcast_to(local, (16, slots)).astype(jnp.bfloat16)
    spot = lax.broadcasted_iota(jnp.int32, (1, half), 1)
    source = (spot // per_half) * (2 * per_half) + rep * per_half + spot % per_half
    hot = (lax.broadcasted_iota(jnp.int32, (slots, half), 0) == source).astype(jnp.bfloat16)
    return dot(local, hot)[:1].astype(jnp.int32)


def convolve_kernel(points_ref, neighbours_ref, taps_ref, acc_ref, window):
    half = acc_ref.shape[0]
    span = half + RIM
    rep = lax.axis_index("rep")
    base = pl.multiple_of(rep * half, half)
    start = pl.multiple_of(rep * (points_ref.shape[0] - span), RIM)
    window[...] = points_ref[pl.ds(start, span)]
    index = (neighbours_ref[:, pl.ds(base, half)] - (RIM + start)).T
    spots = lax.broadcasted_iota(jnp.int32, (half, span), 1)
    for tap in range(taps_ref.shape[0]):
        hot = (spots == index[:, tap : tap + 1]).astype(jnp.bfloat16)
        term = dot(hot, window[...]) * taps_ref[tap : tap + 1, :].astype(jnp.float32)
        if tap == 0:
            acc_ref[...] = term
        else:
            acc_ref[...] += term


def encode_kernel(
    per_half, counts_ref, before_ref, points_ref, after_ref, neighbours_ref, order_ref, taps_ref,
    own_ref, linear_own_ref, linear_other_ref, cpe_gain_ref, attn_gain_ref,
    stream_ref, send_ref,
    acc, encoded,
):
    rows, half = points_ref.shape[0], stream_ref.shape[0]
    rep = lax.axis_index("rep")
    live = counts_ref[0]
    base = pl.multiple_of(rep * half, half)
    acc[...] = own_ref[...]
    index = neighbours_ref[:, pl.ds(base, half)].T
    spots = lax.broadcasted_iota(jnp.int32, (RIM, RIM), 1)

    def add_rim(at, rim_ref, offset):
        piece = index[at : at + RIM] - offset
        for tap in range(taps_ref.shape[0]):
            hot = (spots == piece[:, tap : tap + 1]).astype(jnp.bfloat16)
            acc[at : at + RIM] += dot(hot, rim_ref[...]) * taps_ref[tap : tap + 1, :].astype(jnp.float32)

    for at in range(0, half, RIM):
        if at < RIM:
            pl.when(rep == 0)(lambda at=at: add_rim(at, before_ref, 0))
        first = base + at
        reach = (first < live) & (first + 2 * RIM > live)
        pl.when(reach)(lambda at=at: add_rim(at, after_ref, RIM + rows))
    convolved = acc[...].astype(jnp.bfloat16)
    columns = linear_own_ref.shape[1]
    own_at = pl.multiple_of(rep * columns, columns)
    other_at = pl.multiple_of((1 - rep) * columns, columns)
    encoded[:, pl.ds(own_at, columns)] = dot(convolved, linear_own_ref[...])
    encoded[:, pl.ds(other_at, columns)] = dot(convolved, linear_other_ref[...])
    rounded = encoded[...].astype(jnp.bfloat16).astype(jnp.float32)
    own_points = points_ref[pl.ds(base, half)].astype(jnp.float32)
    stream = own_points + normalize(rounded, cpe_gain_ref[...])
    stream_ref[...] = stream
    normed = normalize(stream, attn_gain_ref[...])
    row = lax.broadcasted_iota(jnp.int32, normed.shape, 0) + base
    marked = jnp.where(row < live, normed, DEAD_MARK).astype(jnp.bfloat16)
    source = lax.broadcasted_iota(jnp.int32, (half, half), 0) + base
    hot = (source - base == own_order(order_ref, base, rep, half, per_half)).astype(jnp.bfloat16)
    send_ref[...] = dot_first(hot, marked).astype(jnp.bfloat16)


def start_copies(sources, targets, semaphores):
    copies = [
        pltpu.make_async_copy(source, target, semaphores.at[at])
        for at, (source, target) in enumerate(zip(sources, targets))
    ]
    for copy in copies:
        copy.start()
    return copies


def attend_kernel(
    own_ref, other_ref, weight_own_hbm, weight_other_hbm, out_ref,
    feats, dead_block, weight_own_ref, weight_other_ref, semaphores,
):
    copies = start_copies(
        (weight_own_hbm, weight_other_hbm), (weight_own_ref, weight_other_ref), semaphores
    )
    half = own_ref.shape[0]
    group_heads = LANES // HEAD_DIM
    lane = lax.broadcasted_iota(jnp.int32, (2 * half, LANES), 1)
    for at, ref in ((0, own_ref), (half, other_ref)):
        rows = ref[...].astype(jnp.float32)
        dead = rows > DEAD_LEVEL
        feats[at : at + half] = jnp.where(dead, 0.0, rows).astype(jnp.bfloat16)
        dead_block[at : at + half] = jnp.where(
            dead[:, :LANES] & (lane[:half] == 0), MASKED, 0.0
        ).astype(jnp.bfloat16)
    first = (lane[:half] == 0).astype(jnp.bfloat16)
    width = own_ref.shape[1]
    work = []
    for side, weight_ref in enumerate((weight_own_ref, weight_other_ref)):
        columns = weight_ref.shape[2]
        copies[side].wait()
        queries = dot(feats[:half], weight_ref[0]).astype(jnp.bfloat16) * (HEAD_DIM ** -0.5)
        queries = queries.astype(jnp.bfloat16)
        keys = dot(feats[...], weight_ref[1]).astype(jnp.bfloat16)
        values = dot(feats[...], weight_ref[2]).astype(jnp.bfloat16)
        work.append((queries, keys, values))
    heads = width // HEAD_DIM

    def score(head):
        queries, keys, _ = work[head * HEAD_DIM // columns]
        at = head * HEAD_DIM % columns // LANES * LANES
        mine = lane // HEAD_DIM == head % group_heads
        key = jnp.where(mine, keys[:, at : at + LANES], 0.0).astype(jnp.bfloat16)
        query = jnp.concatenate([queries[:, at : at + LANES], first], axis=1)
        return dot_last(query, jnp.concatenate([key, dead_block[...]], axis=1))

    def weigh(head, exponent):
        values = work[head * HEAD_DIM // columns][2]
        at = head * HEAD_DIM % columns // LANES * LANES
        mine = lane // HEAD_DIM == head % group_heads
        value = jnp.where(mine, values[:, at : at + LANES], 0.0).astype(jnp.bfloat16)
        return dot(exponent, jnp.concatenate([value, mine.astype(jnp.bfloat16)], axis=1))

    scores = score(0)
    total = pending = None
    for head in range(heads + 1):
        following = score(head + 1) if head + 1 < heads else None
        if pending is not None:
            term = weigh(head - 1, pending)
            total = term if (head - 1) % group_heads == 0 else total + term
            if head % group_heads == 0:
                out_ref[:, (head - group_heads) * HEAD_DIM : head * HEAD_DIM] = (
                    total[:, :LANES] / total[:, LANES:]
                ).astype(jnp.bfloat16)
        if head < heads:
            exponent = jnp.exp(scores - jnp.max(scores, axis=1, keepdims=True))
            pending = exponent.astype(jnp.bfloat16)
        scores = following


def mix_kernel(
    per_half, counts_ref, returned_ref, order_ref, gain_ref, stream_hbm, *refs,
):
    weights, mixed_ref = refs[:6], refs[6]
    stream_ref, out_own_ref, out_other_ref, up_own_ref, up_other_ref, down_ref = refs[7:13]
    semaphores, hidden = refs[13:]
    size = up_own_ref.shape[1]
    copies = start_copies(
        (stream_hbm, *weights),
        (
            stream_ref, out_own_ref, out_other_ref, up_own_ref, up_other_ref,
            down_ref.at[:size], down_ref.at[size:],
        ),
        semaphores,
    )
    half = returned_ref.shape[0]
    columns = out_own_ref.shape[0]
    rep = lax.axis_index("rep")
    live = counts_ref[0]
    base = rep * half
    row = lax.broadcasted_iota(jnp.int32, (half, half), 0)
    hot = (row == own_order(order_ref, base, rep, half, per_half)).astype(jnp.bfloat16)
    restored = dot(hot, returned_ref[...]).astype(jnp.bfloat16)
    for copy in copies[:3]:
        copy.wait()
    mid = (
        stream_ref[...]
        + dot(restored[:, :columns], out_own_ref[...])
        + dot(restored[:, columns:], out_other_ref[...])
    )
    mlp_in = normalize(mid, gain_ref[...]).astype(jnp.bfloat16)
    chunk = min(size, 512)
    for side, up_ref in enumerate((up_own_ref, up_other_ref)):
        copies[3 + side].wait()
        for at in range(0, size, chunk):
            lifted = dot(mlp_in, up_ref[:, at : at + chunk])
            hidden[:, side * size + at : side * size + at + chunk] = gelu(lifted).astype(jnp.bfloat16)
    copies[5].wait()
    copies[6].wait()
    mixed = mid + dot(hidden[...], down_ref[...])
    row = lax.broadcasted_iota(jnp.int32, mixed.shape, 0) + base
    mixed_ref[...] = jnp.where(row < live, mixed, 0.0).astype(jnp.bfloat16)


def call(kernel, out_shape, ins, scratch, flops, transcendentals, limit):
    bytes_accessed = 4 * MIB
    return pl.pallas_call(
        kernel,
        out_shape=out_shape,
        in_specs=ins,
        out_specs=jax.tree.map(lambda _: VMEM, out_shape),
        scratch_shapes=scratch,
        compiler_params=pltpu.CompilerParams(vmem_limit_bytes=limit),
        cost_estimate=pl.CostEstimate(
            flops=flops, bytes_accessed=bytes_accessed, transcendentals=transcendentals
        ),
    )


def shards(
    points,
    counts,
    neighbours,
    order_send,
    cpe_taps,
    cpe_linear,
    cpe_gain,
    attn_gain,
    qkv_weight,
    out_weight,
    mlp_gain,
    up_weight,
    down_weight,
):
    rows, width = points.shape
    half = rows // 2
    taps = neighbours.shape[0]
    ring = ("seg", "ord")
    peers = lax.axis_size("seg") * lax.axis_size("ord")
    per_peer = rows // peers
    per_half = per_peer // 2
    live = counts[0]

    def swap(array):
        return lax.ppermute(array, "rep", [(0, 1), (1, 0)])

    up_hop = [(i, i + 1) for i in range(peers - 1)]
    down_hop = [(i + 1, i) for i in range(peers - 1)]
    after = lax.ppermute(points[:RIM], ring, down_hop)
    before = lax.ppermute(lax.dynamic_slice_in_dim(points, live - RIM, RIM, 0), ring, up_hop)
    linear_other = swap(cpe_linear)
    qkv_own = qkv_weight.transpose(1, 0, 2)
    qkv_other = swap(qkv_own)
    out_other = swap(out_weight)
    up_other = swap(up_weight)
    down_other = swap(down_weight)
    tapping = 2 * taps * half * width
    convolved = call(
        convolve_kernel,
        jax.ShapeDtypeStruct((half, width), jnp.float32),
        [VMEM] * 3,
        [pltpu.VMEM((half + RIM, width), jnp.bfloat16)],
        tapping * (half + RIM),
        0,
        12 * MIB,
    )(points, neighbours, cpe_taps)
    stream, send = call(
        functools.partial(encode_kernel, per_half),
        [
            jax.ShapeDtypeStruct((half, width), jnp.float32),
            jax.ShapeDtypeStruct((half, width), jnp.bfloat16),
        ],
        [SMEM] + [VMEM] * 11,
        [
            pltpu.VMEM((half, width), jnp.float32),
            pltpu.VMEM((half, width), jnp.float32),
        ],
        tapping * RIM,
        half * 4,
        12 * MIB,
    )(
        counts, before, points, after, neighbours, order_send, cpe_taps, convolved,
        cpe_linear, linear_other, cpe_gain.reshape(1, width), attn_gain.reshape(1, width),
    )

    arrived = lax.all_to_all(
        send.reshape(peers, per_half, width), ring, split_axis=0, concat_axis=0, tiled=True
    ).reshape(half, width)
    arrived_other = swap(arrived)
    attended = call(
        attend_kernel,
        jax.ShapeDtypeStruct((half, width), jnp.bfloat16),
        [VMEM] * 2 + [HBM] * 2,
        [pltpu.VMEM((rows, width), jnp.bfloat16), pltpu.VMEM((rows, LANES), jnp.bfloat16)]
        + [pltpu.VMEM(qkv_own.shape, jnp.bfloat16)] * 2
        + [pltpu.SemaphoreType.DMA((2,))],
        2 * (width // HEAD_DIM) * half * rows * 512,
        (width // HEAD_DIM) * half * rows,
        24 * MIB,
    )(arrived, arrived_other, qkv_own, qkv_other)
    returned = lax.all_to_all(
        attended.reshape(peers, per_half, width), ring, split_axis=0, concat_axis=0, tiled=True
    ).reshape(half, width)
    hidden = 2 * up_weight.shape[1]
    weights = (out_weight, out_other, up_weight, up_other, down_weight, down_other)
    return call(
        functools.partial(mix_kernel, per_half),
        jax.ShapeDtypeStruct((half, width), jnp.bfloat16),
        [SMEM] + [VMEM] * 3 + [HBM] * 7,
        [pltpu.VMEM(stream.shape, stream.dtype)]
        + [pltpu.VMEM(weight.shape, weight.dtype) for weight in weights[:4]]
        + [
            pltpu.VMEM((hidden, width), down_weight.dtype),
            pltpu.SemaphoreType.DMA((7,)),
            pltpu.VMEM((half, hidden), jnp.bfloat16),
        ],
        2 * half * width * (width + half + 2 * hidden),
        half * hidden,
        60 * MIB,
    )(counts, returned, order_send, mlp_gain.reshape(1, width), stream, *weights)


def solution(mesh):
    placed = (
        P(("tile", "seg", "ord"), None),
        P(("tile", "seg", "ord")),
        P(None, ("tile", "seg", "ord")),
        P(("tile", "seg", "ord"), None),
        P(),
        P(None, "rep"),
        P(),
        P(),
        P(None, None, "rep"),
        P("rep", None),
        P(),
        P(None, "rep"),
        P("rep", None),
    )
    return jax.shard_map(
        shards,
        mesh=mesh,
        in_specs=placed,
        out_specs=P(("tile", "seg", "ord", "rep"), None),
        check_vma=False,
    )
```

```python
import functools

import jax
import jax.numpy as jnp
from jax import lax
from jax.experimental import pallas as pl
from jax.experimental.pallas import tpu as pltpu
from jax.sharding import PartitionSpec as P

RIM = 128
HEAD_DIM = 16
LANES = 128
TILE = 8
STACK = 4
EPSILON = 1e-06
MASKED = -1e30
DEAD_MARK = 16384.0
DEAD_LEVEL = 8192.0

VMEM = pl.BlockSpec(memory_space=pltpu.VMEM)
SMEM = pl.BlockSpec(memory_space=pltpu.SMEM)
HBM = pl.BlockSpec(memory_space=pltpu.HBM)
MIB = 1 << 20


def dot(a, b):
    return jnp.dot(a, b, preferred_element_type=jnp.float32)


def dot_first(a, b):
    return lax.dot_general(a, b, (((0,), (0,)), ((), ())), preferred_element_type=jnp.float32)


def dot_last(a, b):
    return lax.dot_general(a, b, (((1,), (1,)), ((), ())), preferred_element_type=jnp.float32)


def normalize(values, gain):
    centred = values - jnp.mean(values, axis=-1, keepdims=True)
    spread = jnp.mean(centred * centred, axis=-1, keepdims=True)
    return centred * lax.rsqrt(spread + EPSILON) * gain


def gelu(x):
    return 0.5 * x * (1.0 + jnp.tanh((2.0 / jnp.pi) ** 0.5 * (x + 0.044715 * (x * x * x))))


def own_order(order_ref, base, rep, half, per_half):
    slots = order_ref.shape[1]
    local = jnp.clip(order_ref[...] - base, 0, half - 1).astype(jnp.float32)
    local = jnp.broadcast_to(local, (16, slots)).astype(jnp.bfloat16)
    spot = lax.broadcasted_iota(jnp.int32, (1, half), 1)
    source = (spot // per_half) * (2 * per_half) + rep * per_half + spot % per_half
    hot = (lax.broadcasted_iota(jnp.int32, (slots, half), 0) == source).astype(jnp.bfloat16)
    return dot(local, hot)[:1].astype(jnp.int32)


def add_taps(acc_ref, at, rows, index_ref, offset, source, taps_ref):
    index = index_ref[pl.ds(at, rows)] - offset
    spots = lax.broadcasted_iota(jnp.int32, (rows, source.shape[0]), 1)
    for tap in range(1, taps_ref.shape[0]):
        hot = (spots == index[:, tap : tap + 1]).astype(jnp.bfloat16)
        acc_ref[pl.ds(at, rows)] += dot(hot, source) * taps_ref[tap : tap + 1, :]


def convolve_kernel(points_ref, neighbours_ref, taps_ref, acc_ref, index_ref):
    half = acc_ref.shape[0]
    rep = lax.axis_index("rep")
    base = pl.multiple_of(rep * half, half)
    index_ref[...] = neighbours_ref[...].T
    acc_ref[...] = points_ref[pl.ds(base, half)].astype(jnp.float32) * taps_ref[:1]
    edge = pl.multiple_of(rep * RIM, RIM)
    add_taps(acc_ref, edge, RIM, index_ref, RIM + base, points_ref[pl.ds(base, half)], taps_ref)
    inner = pl.multiple_of((1 - rep) * RIM, RIM)
    start = pl.multiple_of(rep * RIM, RIM)
    span = half + RIM
    add_taps(acc_ref, inner, RIM, index_ref, RIM + start, points_ref[pl.ds(start, span)], taps_ref)


def encode_kernel(
    per_half, counts_ref, before_ref, points_ref, after_ref, neighbours_ref, order_ref, taps_ref,
    own_ref, linear_own_ref, linear_other_ref, cpe_gain_ref, attn_gain_ref, mlp_gain_ref,
    stream_ref, send_ref,
    acc, encoded, index_ref,
):
    rows, half = points_ref.shape[0], send_ref.shape[0]
    rep = lax.axis_index("rep")
    live = counts_ref[0]
    base = pl.multiple_of(rep * half, half)
    acc[...] = own_ref[...]
    index_ref[...] = neighbours_ref[...].T

    @pl.when(rep == 0)
    def _():
        add_taps(acc, 0, RIM, index_ref, 0, before_ref[...], taps_ref)

    reach = live - RIM - base

    @pl.when((reach > -RIM) & (reach < half))
    def _():
        span = RIM + TILE
        at = pl.multiple_of(jnp.clip(reach // TILE * TILE, 0, half - span), TILE)
        add_taps(acc, at, span, index_ref, RIM + rows, after_ref[...], taps_ref)

    convolved = acc[...].astype(jnp.bfloat16)
    columns = linear_own_ref.shape[1]
    own_at = pl.multiple_of(rep * columns, columns)
    other_at = pl.multiple_of((1 - rep) * columns, columns)
    encoded[:, pl.ds(own_at, columns)] = dot(convolved, linear_own_ref[...])
    encoded[:, pl.ds(other_at, columns)] = dot(convolved, linear_other_ref[...])
    rounded = encoded[...].astype(jnp.bfloat16).astype(jnp.float32)
    own_points = points_ref[pl.ds(base, half)].astype(jnp.float32)
    stream = own_points + normalize(rounded, cpe_gain_ref[...])
    stream_ref[:half] = stream
    normed = normalize(stream, attn_gain_ref[...])
    row = lax.broadcasted_iota(jnp.int32, normed.shape, 0) + base
    marked = jnp.where(row < live, normed, DEAD_MARK).astype(jnp.bfloat16)
    source = lax.broadcasted_iota(jnp.int32, (half, half), 0) + base
    order = own_order(order_ref, base, rep, half, per_half)
    hot = (source - base == order).astype(jnp.bfloat16)
    send_ref[...] = dot_first(hot, marked).astype(jnp.bfloat16)
    stream_ref[half : half + 1] = mlp_gain_ref[...]
    stream_ref[half + 1 : half + 2, :half] = order.astype(jnp.float32)


def start_copies(sources, targets, semaphores):
    copies = [
        pltpu.make_async_copy(source, target, semaphores.at[at])
        for at, (source, target) in enumerate(zip(sources, targets))
    ]
    for copy in copies:
        copy.start()
    return copies


def attend_kernel(
    own_ref, other_ref, weight_own_hbm, weight_other_hbm, out_ref,
    feats, dead_block, weight_own_ref, weight_other_ref, semaphores,
):
    copies = start_copies(
        (weight_own_hbm, weight_other_hbm), (weight_own_ref, weight_other_ref), semaphores
    )
    half = own_ref.shape[0]
    group_heads = LANES // HEAD_DIM
    lane = lax.broadcasted_iota(jnp.int32, (2 * half, LANES), 1)
    for at, ref in ((0, own_ref), (half, other_ref)):
        rows = ref[...].astype(jnp.float32)
        dead = rows > DEAD_LEVEL
        feats[at : at + half] = jnp.where(dead, 0.0, rows).astype(jnp.bfloat16)
        dead_block[at : at + half] = jnp.where(
            dead[:, :LANES] & (lane[:half] == 0), MASKED, 0.0
        ).astype(jnp.bfloat16)
    first = (lane[:half] == 0).astype(jnp.bfloat16)
    width = own_ref.shape[1]
    work = []
    for side, weight_ref in enumerate((weight_own_ref, weight_other_ref)):
        columns = weight_ref.shape[2]
        copies[side].wait()
        queries = dot(feats[:half], weight_ref[0]).astype(jnp.bfloat16) * (HEAD_DIM ** -0.5)
        queries = queries.astype(jnp.bfloat16)
        keys = dot(feats[...], weight_ref[1]).astype(jnp.bfloat16)
        values = dot(feats[...], weight_ref[2]).astype(jnp.bfloat16)
        work.append((queries, keys, values))
    stacks = width // HEAD_DIM // STACK

    def place(stack):
        at = stack * STACK * HEAD_DIM
        return work[at // columns], at % columns // LANES * LANES, at % LANES // HEAD_DIM

    def score(stack):
        (queries, keys, _), at, lowest = place(stack)
        query = jnp.concatenate(
            [
                jnp.where(lane[:half] // HEAD_DIM == lowest + head, queries[:, at : at + LANES], 0.0)
                for head in range(STACK)
            ],
            axis=0,
        ).astype(jnp.bfloat16)
        query = jnp.concatenate([query, jnp.concatenate([first] * STACK, axis=0)], axis=1)
        return dot_last(query, jnp.concatenate([keys[:, at : at + LANES], dead_block[...]], axis=1))

    def weigh(stack, exponent):
        (_, _, values), at, _ = place(stack)
        return dot(
            exponent, jnp.concatenate([values[:, at : at + LANES], jnp.ones(dead_block.shape, jnp.bfloat16)], axis=1)
        )

    scores = score(0)
    total = pending = None
    for stack in range(stacks + 1):
        following = score(stack + 1) if stack + 1 < stacks else None
        if pending is not None:
            result = weigh(stack - 1, pending)
            _, at, lowest = place(stack - 1)
            for head in range(STACK):
                piece = result[head * half : (head + 1) * half]
                piece = piece[:, :LANES] / piece[:, LANES:]
                mine = lane[:half] // HEAD_DIM == lowest + head
                total = piece if lowest + head == 0 else jnp.where(mine, piece, total)
            if lowest + STACK == group_heads:
                end = stack * STACK * HEAD_DIM
                out_ref[:, end - LANES : end] = total.astype(jnp.bfloat16)
        if stack < stacks:
            exponent = jnp.exp(scores - jnp.max(scores, axis=1, keepdims=True))
            pending = exponent.astype(jnp.bfloat16)
        scores = following


def mix_kernel(
    counts_ref, returned_hbm, stream_hbm, *refs,
):
    weights, mixed_ref = refs[:6], refs[6]
    stream_ref, returned_ref = refs[7:9]
    out_own_ref, out_other_ref, up_own_ref, up_other_ref, down_ref, semaphores, hidden = refs[9:]
    size = up_own_ref.shape[1]
    copies = start_copies(
        (stream_hbm, returned_hbm, *weights),
        (
            stream_ref, returned_ref, out_own_ref, out_other_ref, up_own_ref, up_other_ref,
            down_ref.at[:size], down_ref.at[size:],
        ),
        semaphores,
    )
    half = returned_ref.shape[0]
    columns = out_own_ref.shape[0]
    rep = lax.axis_index("rep")
    live = counts_ref[0]
    base = rep * half
    row = lax.broadcasted_iota(jnp.int32, (half, half), 0)
    copies[0].wait()
    hot = (row == stream_ref[half + 1 : half + 2, :half].astype(jnp.int32)).astype(jnp.bfloat16)
    copies[1].wait()
    restored = dot(hot, returned_ref[...]).astype(jnp.bfloat16)
    copies[2].wait()
    copies[3].wait()
    mid = (
        stream_ref[:half]
        + dot(restored[:, :columns], out_own_ref[...])
        + dot(restored[:, columns:], out_other_ref[...])
    )
    mlp_in = normalize(mid, stream_ref[half : half + 1]).astype(jnp.bfloat16)
    chunk = min(size, 512)
    for side, up_ref in enumerate((up_own_ref, up_other_ref)):
        copies[4 + side].wait()
        for at in range(0, size, chunk):
            lifted = dot(mlp_in, up_ref[:, at : at + chunk])
            hidden[:, side * size + at : side * size + at + chunk] = gelu(lifted).astype(jnp.bfloat16)
    copies[6].wait()
    copies[7].wait()
    mixed = mid + dot(hidden[...], down_ref[...])
    row = lax.broadcasted_iota(jnp.int32, mixed.shape, 0) + base
    mixed_ref[...] = jnp.where(row < live, mixed, 0.0).astype(jnp.bfloat16)


def call(kernel, out_shape, ins, scratch, flops, transcendentals, limit):
    bytes_accessed = 4 * MIB
    return pl.pallas_call(
        kernel,
        out_shape=out_shape,
        in_specs=ins,
        out_specs=jax.tree.map(lambda _: VMEM, out_shape),
        scratch_shapes=scratch,
        compiler_params=pltpu.CompilerParams(vmem_limit_bytes=limit),
        cost_estimate=pl.CostEstimate(
            flops=flops, bytes_accessed=bytes_accessed, transcendentals=transcendentals
        ),
    )


def shards(
    points,
    counts,
    neighbours,
    order_send,
    cpe_taps,
    cpe_linear,
    cpe_gain,
    attn_gain,
    qkv_weight,
    out_weight,
    mlp_gain,
    up_weight,
    down_weight,
):
    rows, width = points.shape
    half = rows // 2
    taps = neighbours.shape[0]
    ring = ("seg", "ord")
    peers = lax.axis_size("seg") * lax.axis_size("ord")
    per_peer = rows // peers
    per_half = per_peer // 2
    live = counts[0]

    def swap(array):
        return lax.ppermute(array, "rep", [(0, 1), (1, 0)])

    up_hop = [(i, i + 1) for i in range(peers - 1)]
    down_hop = [(i + 1, i) for i in range(peers - 1)]
    after = lax.ppermute(points[:RIM], ring, down_hop)
    before = lax.ppermute(lax.dynamic_slice_in_dim(points, live - RIM, RIM, 0), ring, up_hop)
    linear_other = swap(cpe_linear)
    qkv_own = qkv_weight.transpose(1, 0, 2)
    qkv_other = swap(qkv_own)
    out_other = swap(out_weight)
    up_other = swap(up_weight)
    down_other = swap(down_weight)
    tapping = 2 * taps * half * width
    tap_rows = cpe_taps.astype(jnp.float32)
    rep = lax.axis_index("rep")
    own_neighbours = lax.dynamic_slice_in_dim(neighbours, rep * half, half, 1)
    convolved = call(
        convolve_kernel,
        jax.ShapeDtypeStruct((half, width), jnp.float32),
        [VMEM] * 3,
        [pltpu.VMEM((half, taps), jnp.int32)],
        tapping * (half + RIM),
        0,
        12 * MIB,
    )(points, own_neighbours, tap_rows)
    stream, send = call(
        functools.partial(encode_kernel, per_half),
        [
            jax.ShapeDtypeStruct((half + TILE, width), jnp.float32),
            jax.ShapeDtypeStruct((half, width), jnp.bfloat16),
        ],
        [SMEM] + [VMEM] * 12,
        [
            pltpu.VMEM((half, width), jnp.float32),
            pltpu.VMEM((half, width), jnp.float32),
            pltpu.VMEM((half, taps), jnp.int32),
        ],
        tapping * RIM,
        half * 4,
        12 * MIB,
    )(
        counts, before, points, after, own_neighbours, order_send, tap_rows, convolved,
        cpe_linear, linear_other, cpe_gain.reshape(1, width), attn_gain.reshape(1, width),
        mlp_gain.reshape(1, width),
    )

    arrived = lax.all_to_all(
        send.reshape(peers, per_half, width), ring, split_axis=0, concat_axis=0, tiled=True
    ).reshape(half, width)
    arrived_other = swap(arrived)
    attended = call(
        attend_kernel,
        jax.ShapeDtypeStruct((half, width), jnp.bfloat16),
        [VMEM] * 2 + [HBM] * 2,
        [pltpu.VMEM((rows, width), jnp.bfloat16), pltpu.VMEM((rows, LANES), jnp.bfloat16)]
        + [pltpu.VMEM(qkv_own.shape, jnp.bfloat16)] * 2
        + [pltpu.SemaphoreType.DMA((2,))],
        2 * (width // HEAD_DIM) * half * rows * 512,
        (width // HEAD_DIM) * half * rows,
        32 * MIB,
    )(arrived, arrived_other, qkv_own, qkv_other)
    returned = lax.all_to_all(
        attended.reshape(peers, per_half, width), ring, split_axis=0, concat_axis=0, tiled=True
    ).reshape(half, width)
    hidden = 2 * up_weight.shape[1]
    weights = (out_weight, out_other, up_weight, up_other, down_weight, down_other)
    return call(
        mix_kernel,
        jax.ShapeDtypeStruct((half, width), jnp.bfloat16),
        [SMEM] + [HBM] * 8,
        [pltpu.VMEM(array.shape, array.dtype) for array in (stream, returned, *weights[:4])]
        + [
            pltpu.VMEM((hidden, width), down_weight.dtype),
            pltpu.SemaphoreType.DMA((8,)),
            pltpu.VMEM((half, hidden), jnp.bfloat16),
        ],
        2 * half * width * (width + half + 2 * hidden),
        half * hidden,
        52 * MIB,
    )(counts, returned, stream, *weights)


def solution(mesh):
    placed = (
        P(("tile", "seg", "ord"), None),
        P(("tile", "seg", "ord")),
        P(None, ("tile", "seg", "ord")),
        P(("tile", "seg", "ord"), None),
        P(),
        P(None, "rep"),
        P(),
        P(),
        P(None, None, "rep"),
        P("rep", None),
        P(),
        P(None, "rep"),
        P("rep", None),
    )
    return jax.shard_map(
        shards,
        mesh=mesh,
        in_specs=placed,
        out_specs=P(("tile", "seg", "ord", "rep"), None),
        check_vma=False,
    )
```

```python
import functools

import jax
import jax.numpy as jnp
from jax import lax
from jax.experimental import pallas as pl
from jax.experimental.pallas import tpu as pltpu
from jax.sharding import PartitionSpec as P

RIM = 128
HEAD_DIM = 16
LANES = 128
TILE = 8
STACK = 2
EPSILON = 1e-06
MASKED = -1e30
DEAD_MARK = 16384.0
DEAD_LEVEL = 8192.0

VMEM = pl.BlockSpec(memory_space=pltpu.VMEM)
SMEM = pl.BlockSpec(memory_space=pltpu.SMEM)
HBM = pl.BlockSpec(memory_space=pltpu.HBM)
MIB = 1 << 20


def dot(a, b):
    return jnp.dot(a, b, preferred_element_type=jnp.float32)


def dot_first(a, b):
    return lax.dot_general(a, b, (((0,), (0,)), ((), ())), preferred_element_type=jnp.float32)


def dot_last(a, b):
    return lax.dot_general(a, b, (((1,), (1,)), ((), ())), preferred_element_type=jnp.float32)


def normalize(values, gain):
    centred = values - jnp.mean(values, axis=-1, keepdims=True)
    spread = jnp.mean(centred * centred, axis=-1, keepdims=True)
    return centred * lax.rsqrt(spread + EPSILON) * gain


def gelu(x):
    return 0.5 * x * (1.0 + jnp.tanh((2.0 / jnp.pi) ** 0.5 * (x + 0.044715 * (x * x * x))))


def own_order(order, base, rep, half, per_half):
    slots = order.shape[1]
    local = jnp.clip(order - base, 0, half - 1).astype(jnp.float32)
    local = jnp.broadcast_to(local, (16, slots)).astype(jnp.bfloat16)
    spot = lax.broadcasted_iota(jnp.int32, (1, half), 1)
    source = (spot // per_half) * (2 * per_half) + rep * per_half + spot % per_half
    hot = (lax.broadcasted_iota(jnp.int32, (slots, half), 0) == source).astype(jnp.bfloat16)
    return dot(local, hot)[:1].astype(jnp.int32)


def add_taps(acc_ref, at, rows, index_ref, offset, source, taps_ref):
    index = index_ref[pl.ds(at, rows)] - offset
    spots = lax.broadcasted_iota(jnp.int32, (rows, source.shape[0]), 1)
    for tap in range(1, index_ref.shape[1]):
        hot = (spots == index[:, tap : tap + 1]).astype(jnp.bfloat16)
        acc_ref[pl.ds(at, rows)] += dot(hot, source) * taps_ref[tap : tap + 1, :]


def convolve_kernel(points_ref, neighbours_ref, taps_ref, acc_ref, index_ref):
    half = acc_ref.shape[0]
    rep = lax.axis_index("rep")
    base = pl.multiple_of(rep * half, half)
    index_ref[...] = neighbours_ref[...].T
    acc_ref[...] = points_ref[pl.ds(base, half)].astype(jnp.float32) * taps_ref[:1]
    edge = pl.multiple_of(rep * RIM, RIM)
    add_taps(acc_ref, edge, RIM, index_ref, RIM + base, points_ref[pl.ds(base, half)], taps_ref)
    inner = pl.multiple_of((1 - rep) * RIM, RIM)
    start = pl.multiple_of(rep * RIM, RIM)
    span = half + RIM
    add_taps(acc_ref, inner, RIM, index_ref, RIM + start, points_ref[pl.ds(start, span)], taps_ref)


def encode_kernel(
    per_half, counts_ref, before_ref, points_ref, after_ref, neighbours_ref, taps_ref,
    own_ref, linear_own_ref, linear_other_ref, cpe_gain_ref, attn_gain_ref, mlp_gain_ref,
    stream_ref, send_ref,
    acc, encoded, index_ref,
):
    rows, half = points_ref.shape[0], send_ref.shape[0]
    rep = lax.axis_index("rep")
    live = counts_ref[0]
    base = pl.multiple_of(rep * half, half)
    acc[...] = own_ref[...]
    index_ref[...] = neighbours_ref[...].T

    @pl.when(rep == 0)
    def _():
        add_taps(acc, 0, RIM, index_ref, 0, before_ref[...], taps_ref)

    reach = live - RIM - base

    @pl.when((reach > -RIM) & (reach < half))
    def _():
        span = RIM + TILE
        at = pl.multiple_of(jnp.clip(reach // TILE * TILE, 0, half - span), TILE)
        add_taps(acc, at, span, index_ref, RIM + rows, after_ref[...], taps_ref)

    convolved = acc[...].astype(jnp.bfloat16)
    columns = linear_own_ref.shape[1]
    own_at = pl.multiple_of(rep * columns, columns)
    other_at = pl.multiple_of((1 - rep) * columns, columns)
    encoded[:, pl.ds(own_at, columns)] = dot(convolved, linear_own_ref[...])
    encoded[:, pl.ds(other_at, columns)] = dot(convolved, linear_other_ref[...])
    rounded = encoded[...].astype(jnp.bfloat16).astype(jnp.float32)
    own_points = points_ref[pl.ds(base, half)].astype(jnp.float32)
    stream = own_points + normalize(rounded, cpe_gain_ref[...])
    stream_ref[:half] = stream
    normed = normalize(stream, attn_gain_ref[...])
    row = lax.broadcasted_iota(jnp.int32, normed.shape, 0) + base
    marked = jnp.where(row < live, normed, DEAD_MARK).astype(jnp.bfloat16)
    source = lax.broadcasted_iota(jnp.int32, (half, half), 0) + base
    taps = neighbours_ref.shape[0]
    order = own_order(taps_ref[taps : taps + 1].astype(jnp.int32), base, rep, half, per_half)
    hot = (source - base == order).astype(jnp.bfloat16)
    send_ref[...] = dot_first(hot, marked).astype(jnp.bfloat16)
    stream_ref[half : half + 1] = mlp_gain_ref[...]
    stream_ref[half + 1 : half + 2, :half] = order.astype(jnp.float32)


def start_copies(sources, targets, semaphores):
    copies = [
        pltpu.make_async_copy(source, target, semaphores.at[at])
        for at, (source, target) in enumerate(zip(sources, targets))
    ]
    for copy in copies:
        copy.start()
    return copies


def attend_kernel(
    own_ref, other_ref, weight_own_hbm, weight_other_hbm, out_ref,
    feats, dead_block, weight_own_ref, weight_other_ref, semaphores,
):
    copies = start_copies(
        (weight_own_hbm, weight_other_hbm), (weight_own_ref, weight_other_ref), semaphores
    )
    half = own_ref.shape[0]
    group_heads = LANES // HEAD_DIM
    lane = lax.broadcasted_iota(jnp.int32, (2 * half, LANES), 1)
    for at, ref in ((0, own_ref), (half, other_ref)):
        rows = ref[...].astype(jnp.float32)
        dead = rows > DEAD_LEVEL
        feats[at : at + half] = jnp.where(dead, 0.0, rows).astype(jnp.bfloat16)
        dead_block[at : at + half] = jnp.where(
            dead[:, :LANES] & (lane[:half] == 0), MASKED, 0.0
        ).astype(jnp.bfloat16)
    first = (lane[:half] == 0).astype(jnp.bfloat16)
    width = own_ref.shape[1]
    work = []
    for side, weight_ref in enumerate((weight_own_ref, weight_other_ref)):
        columns = weight_ref.shape[2]
        copies[side].wait()
        queries = dot(feats[:half], weight_ref[0]).astype(jnp.bfloat16) * (HEAD_DIM ** -0.5)
        queries = queries.astype(jnp.bfloat16)
        keys = dot(feats[...], weight_ref[1]).astype(jnp.bfloat16)
        values = dot(feats[...], weight_ref[2]).astype(jnp.bfloat16)
        work.append((queries, keys, values))
    stacks = width // HEAD_DIM // STACK

    def place(stack):
        at = stack * STACK * HEAD_DIM
        return work[at // columns], at % columns // LANES * LANES, at % LANES // HEAD_DIM

    def score(stack):
        (queries, keys, _), at, lowest = place(stack)
        query = jnp.concatenate(
            [
                jnp.where(lane[:half] // HEAD_DIM == lowest + head, queries[:, at : at + LANES], 0.0)
                for head in range(STACK)
            ],
            axis=0,
        ).astype(jnp.bfloat16)
        query = jnp.concatenate([query, jnp.concatenate([first] * STACK, axis=0)], axis=1)
        return dot_last(query, jnp.concatenate([keys[:, at : at + LANES], dead_block[...]], axis=1))

    def weigh(stack, exponent):
        (_, _, values), at, _ = place(stack)
        return dot(
            exponent, jnp.concatenate([values[:, at : at + LANES], jnp.ones(dead_block.shape, jnp.bfloat16)], axis=1)
        )

    scores = score(0)
    total = pending = None
    for stack in range(stacks + 1):
        following = score(stack + 1) if stack + 1 < stacks else None
        if pending is not None:
            result = weigh(stack - 1, pending)
            _, at, lowest = place(stack - 1)
            for head in range(STACK):
                piece = result[head * half : (head + 1) * half]
                piece = piece[:, :LANES] / piece[:, LANES:]
                mine = lane[:half] // HEAD_DIM == lowest + head
                total = piece if lowest + head == 0 else jnp.where(mine, piece, total)
            if lowest + STACK == group_heads:
                end = stack * STACK * HEAD_DIM
                out_ref[:, end - LANES : end] = total.astype(jnp.bfloat16)
        if stack < stacks:
            exponent = jnp.exp(scores - jnp.max(scores, axis=1, keepdims=True))
            pending = exponent.astype(jnp.bfloat16)
        scores = following


def mix_kernel(
    counts_ref, returned_hbm, stream_hbm, *refs,
):
    weights, mixed_ref = refs[:6], refs[6]
    stream_ref, returned_ref = refs[7:9]
    out_own_ref, out_other_ref, up_own_ref, up_other_ref, down_ref, semaphores, hidden = refs[9:]
    size = up_own_ref.shape[1]
    copies = start_copies(
        (stream_hbm, returned_hbm, *weights),
        (
            stream_ref, returned_ref, out_own_ref, out_other_ref, up_own_ref, up_other_ref,
            down_ref.at[:size], down_ref.at[size:],
        ),
        semaphores,
    )
    half = returned_ref.shape[0]
    columns = out_own_ref.shape[0]
    rep = lax.axis_index("rep")
    live = counts_ref[0]
    base = rep * half
    row = lax.broadcasted_iota(jnp.int32, (half, half), 0)
    copies[0].wait()
    hot = (row == stream_ref[half + 1 : half + 2, :half].astype(jnp.int32)).astype(jnp.bfloat16)
    copies[1].wait()
    restored = dot(hot, returned_ref[...]).astype(jnp.bfloat16)
    copies[2].wait()
    copies[3].wait()
    mid = (
        stream_ref[:half]
        + dot(restored[:, :columns], out_own_ref[...])
        + dot(restored[:, columns:], out_other_ref[...])
    )
    mlp_in = normalize(mid, stream_ref[half : half + 1]).astype(jnp.bfloat16)
    chunk = min(size, 512)
    for side, up_ref in enumerate((up_own_ref, up_other_ref)):
        copies[4 + side].wait()
        for at in range(0, size, chunk):
            lifted = dot(mlp_in, up_ref[:, at : at + chunk])
            hidden[:, side * size + at : side * size + at + chunk] = gelu(lifted).astype(jnp.bfloat16)
    copies[6].wait()
    copies[7].wait()
    mixed = mid + dot(hidden[...], down_ref[...])
    row = lax.broadcasted_iota(jnp.int32, mixed.shape, 0) + base
    mixed_ref[...] = jnp.where(row < live, mixed, 0.0).astype(jnp.bfloat16)


def call(kernel, out_shape, ins, scratch, flops, transcendentals, limit):
    bytes_accessed = 4 * MIB
    return pl.pallas_call(
        kernel,
        out_shape=out_shape,
        in_specs=ins,
        out_specs=jax.tree.map(lambda _: VMEM, out_shape),
        scratch_shapes=scratch,
        compiler_params=pltpu.CompilerParams(vmem_limit_bytes=limit),
        cost_estimate=pl.CostEstimate(
            flops=flops, bytes_accessed=bytes_accessed, transcendentals=transcendentals
        ),
    )


def shards(
    points,
    counts,
    neighbours,
    order_send,
    cpe_taps,
    cpe_linear,
    cpe_gain,
    attn_gain,
    qkv_weight,
    out_weight,
    mlp_gain,
    up_weight,
    down_weight,
):
    rows, width = points.shape
    half = rows // 2
    taps = neighbours.shape[0]
    ring = ("seg", "ord")
    peers = lax.axis_size("seg") * lax.axis_size("ord")
    per_peer = rows // peers
    per_half = per_peer // 2
    live = counts[0]

    def swap(array):
        return lax.ppermute(array, "rep", [(0, 1), (1, 0)])

    up_hop = [(i, i + 1) for i in range(peers - 1)]
    down_hop = [(i + 1, i) for i in range(peers - 1)]
    after = lax.ppermute(points[:RIM], ring, down_hop)
    before = lax.ppermute(lax.dynamic_slice_in_dim(points, live - RIM, RIM, 0), ring, up_hop)
    linear_other = swap(cpe_linear)
    qkv_own = qkv_weight.transpose(1, 0, 2)
    qkv_other = swap(qkv_own)
    out_other = swap(out_weight)
    up_other = swap(up_weight)
    down_other = swap(down_weight)
    tapping = 2 * taps * half * width
    tap_rows = jnp.concatenate([cpe_taps.astype(jnp.float32), order_send.astype(jnp.float32)], axis=0)
    rep = lax.axis_index("rep")
    own_neighbours = lax.dynamic_slice_in_dim(neighbours, rep * half, half, 1)
    convolved = call(
        convolve_kernel,
        jax.ShapeDtypeStruct((half, width), jnp.float32),
        [VMEM] * 3,
        [pltpu.VMEM((half, taps), jnp.int32)],
        tapping * (half + RIM),
        0,
        12 * MIB,
    )(points, own_neighbours, tap_rows)
    stream, send = call(
        functools.partial(encode_kernel, per_half),
        [
            jax.ShapeDtypeStruct((half + TILE, width), jnp.float32),
            jax.ShapeDtypeStruct((half, width), jnp.bfloat16),
        ],
        [SMEM] + [VMEM] * 11,
        [
            pltpu.VMEM((half, width), jnp.float32),
            pltpu.VMEM((half, width), jnp.float32),
            pltpu.VMEM((half, taps), jnp.int32),
        ],
        tapping * RIM,
        half * 4,
        12 * MIB,
    )(
        counts, before, points, after, own_neighbours, tap_rows, convolved,
        cpe_linear, linear_other, cpe_gain.reshape(1, width), attn_gain.reshape(1, width),
        mlp_gain.reshape(1, width),
    )

    arrived = lax.all_to_all(
        send.reshape(peers, per_half, width), ring, split_axis=0, concat_axis=0, tiled=True
    ).reshape(half, width)
    arrived_other = swap(arrived)
    attended = call(
        attend_kernel,
        jax.ShapeDtypeStruct((half, width), jnp.bfloat16),
        [VMEM] * 2 + [HBM] * 2,
        [pltpu.VMEM((rows, width), jnp.bfloat16), pltpu.VMEM((rows, LANES), jnp.bfloat16)]
        + [pltpu.VMEM(qkv_own.shape, jnp.bfloat16)] * 2
        + [pltpu.SemaphoreType.DMA((2,))],
        2 * (width // HEAD_DIM) * half * rows * 512,
        (width // HEAD_DIM) * half * rows,
        32 * MIB,
    )(arrived, arrived_other, qkv_own, qkv_other)
    returned = lax.all_to_all(
        attended.reshape(peers, per_half, width), ring, split_axis=0, concat_axis=0, tiled=True
    ).reshape(half, width)
    hidden = 2 * up_weight.shape[1]
    weights = (out_weight, out_other, up_weight, up_other, down_weight, down_other)
    return call(
        mix_kernel,
        jax.ShapeDtypeStruct((half, width), jnp.bfloat16),
        [SMEM] + [HBM] * 8,
        [pltpu.VMEM(array.shape, array.dtype) for array in (stream, returned, *weights[:4])]
        + [
            pltpu.VMEM((hidden, width), down_weight.dtype),
            pltpu.SemaphoreType.DMA((8,)),
            pltpu.VMEM((half, hidden), jnp.bfloat16),
        ],
        2 * half * width * (width + half + 2 * hidden),
        half * hidden,
        52 * MIB,
    )(counts, returned, stream, *weights)


def solution(mesh):
    placed = (
        P(("tile", "seg", "ord"), None),
        P(("tile", "seg", "ord")),
        P(None, ("tile", "seg", "ord")),
        P(("tile", "seg", "ord"), None),
        P(),
        P(None, "rep"),
        P(),
        P(),
        P(None, None, "rep"),
        P("rep", None),
        P(),
        P(None, "rep"),
        P("rep", None),
    )
    return jax.shard_map(
        shards,
        mesh=mesh,
        in_specs=placed,
        out_specs=P(("tile", "seg", "ord", "rep"), None),
        check_vma=False,
    )
```

```python
import functools

import jax
import jax.numpy as jnp
from jax import lax
from jax.experimental import pallas as pl
from jax.experimental.pallas import tpu as pltpu
from jax.sharding import PartitionSpec as P

RIM = 128
HEAD_DIM = 16
LANES = 128
TILE = 8
STACK = 2
EPSILON = 1e-06
MASKED = -1e30
DEAD_MARK = 16384.0
DEAD_LEVEL = 8192.0

VMEM = pl.BlockSpec(memory_space=pltpu.VMEM)
SMEM = pl.BlockSpec(memory_space=pltpu.SMEM)
HBM = pl.BlockSpec(memory_space=pltpu.HBM)
MIB = 1 << 20


def dot(a, b):
    return jnp.dot(a, b, preferred_element_type=jnp.float32)


def dot_first(a, b):
    return lax.dot_general(a, b, (((0,), (0,)), ((), ())), preferred_element_type=jnp.float32)


def dot_last(a, b):
    return lax.dot_general(a, b, (((1,), (1,)), ((), ())), preferred_element_type=jnp.float32)


def normalize(values, gain):
    centred = values - jnp.mean(values, axis=-1, keepdims=True)
    spread = jnp.mean(centred * centred, axis=-1, keepdims=True)
    return centred * lax.rsqrt(spread + EPSILON) * gain


def gelu(x):
    return 0.5 * x * (1.0 + jnp.tanh((2.0 / jnp.pi) ** 0.5 * (x + 0.044715 * (x * x * x))))


def own_order(order, base, rep, half, per_half):
    slots = order.shape[1]
    local = jnp.clip(order - base, 0, half - 1).astype(jnp.float32)
    local = jnp.broadcast_to(local, (16, slots)).astype(jnp.bfloat16)
    spot = lax.broadcasted_iota(jnp.int32, (1, half), 1)
    source = (spot // per_half) * (2 * per_half) + rep * per_half + spot % per_half
    hot = (lax.broadcasted_iota(jnp.int32, (slots, half), 0) == source).astype(jnp.bfloat16)
    return dot(local, hot)[:1].astype(jnp.int32)


def add_taps(acc_ref, at, rows, index_ref, offset, source, taps_ref):
    index = index_ref[pl.ds(at, rows)] - offset
    spots = lax.broadcasted_iota(jnp.int32, (rows, source.shape[0]), 1)
    for tap in range(1, index_ref.shape[1]):
        hot = (spots == index[:, tap : tap + 1]).astype(jnp.bfloat16)
        acc_ref[pl.ds(at, rows)] += dot(hot, source) * taps_ref[tap : tap + 1, :]


def convolve_kernel(points_ref, neighbours_ref, taps_ref, acc_ref, index_ref):
    half = acc_ref.shape[0]
    rep = lax.axis_index("rep")
    base = pl.multiple_of(rep * half, half)
    index_ref[...] = neighbours_ref[...].T
    acc_ref[...] = points_ref[pl.ds(base, half)].astype(jnp.float32) * taps_ref[:1]
    edge = pl.multiple_of(rep * RIM, RIM)
    add_taps(acc_ref, edge, RIM, index_ref, RIM + base, points_ref[pl.ds(base, half)], taps_ref)
    inner = pl.multiple_of((1 - rep) * RIM, RIM)
    start = pl.multiple_of(rep * RIM, RIM)
    span = half + RIM
    add_taps(acc_ref, inner, RIM, index_ref, RIM + start, points_ref[pl.ds(start, span)], taps_ref)


def encode_kernel(
    per_half, counts_ref, before_ref, points_ref, after_ref, neighbours_ref, taps_ref,
    own_ref, linear_own_ref, linear_other_ref, cpe_gain_ref, attn_gain_ref, mlp_gain_ref,
    stream_ref, send_ref,
    acc, encoded, index_ref,
):
    rows, half = points_ref.shape[0], send_ref.shape[0]
    rep = lax.axis_index("rep")
    live = counts_ref[0]
    base = pl.multiple_of(rep * half, half)
    acc[...] = own_ref[...]
    index_ref[...] = neighbours_ref[...].T

    @pl.when(rep == 0)
    def _():
        add_taps(acc, 0, RIM, index_ref, 0, before_ref[...], taps_ref)

    reach = live - RIM - base

    @pl.when((reach > -RIM) & (reach < half))
    def _():
        span = RIM + TILE
        at = pl.multiple_of(jnp.clip(reach // TILE * TILE, 0, half - span), TILE)
        add_taps(acc, at, span, index_ref, RIM + rows, after_ref[...], taps_ref)

    convolved = acc[...].astype(jnp.bfloat16)
    columns = linear_own_ref.shape[1]
    own_at = pl.multiple_of(rep * columns, columns)
    other_at = pl.multiple_of((1 - rep) * columns, columns)
    encoded[:, pl.ds(own_at, columns)] = dot(convolved, linear_own_ref[...])
    encoded[:, pl.ds(other_at, columns)] = dot(convolved, linear_other_ref[...])
    rounded = encoded[...].astype(jnp.bfloat16).astype(jnp.float32)
    own_points = points_ref[pl.ds(base, half)].astype(jnp.float32)
    stream = own_points + normalize(rounded, cpe_gain_ref[...])
    stream_ref[:half] = stream
    normed = normalize(stream, attn_gain_ref[...])
    row = lax.broadcasted_iota(jnp.int32, normed.shape, 0) + base
    marked = jnp.where(row < live, normed, DEAD_MARK).astype(jnp.bfloat16)
    source = lax.broadcasted_iota(jnp.int32, (half, half), 0) + base
    taps = neighbours_ref.shape[0]
    order = own_order(taps_ref[taps : taps + 1].astype(jnp.int32), base, rep, half, per_half)
    hot = (source - base == order).astype(jnp.bfloat16)
    send_ref[...] = dot_first(hot, marked).astype(jnp.bfloat16)
    stream_ref[half : half + 1] = mlp_gain_ref[...]
    stream_ref[half + 1 : half + 2, :half] = order.astype(jnp.float32)


def start_copies(sources, targets, semaphores):
    copies = [
        pltpu.make_async_copy(source, target, semaphores.at[at])
        for at, (source, target) in enumerate(zip(sources, targets))
    ]
    for copy in copies:
        copy.start()
    return copies


def attend_kernel(
    own_ref, other_ref, weight_own_ref, weight_other_ref, out_ref,
    feats, dead_block,
):
    half = own_ref.shape[0]
    group_heads = LANES // HEAD_DIM
    lane = lax.broadcasted_iota(jnp.int32, (2 * half, LANES), 1)
    for at, ref in ((0, own_ref), (half, other_ref)):
        rows = ref[...].astype(jnp.float32)
        dead = rows > DEAD_LEVEL
        feats[at : at + half] = jnp.where(dead, 0.0, rows).astype(jnp.bfloat16)
        dead_block[at : at + half] = jnp.where(
            dead[:, :LANES] & (lane[:half] == 0), MASKED, 0.0
        ).astype(jnp.bfloat16)
    first = (lane[:half] == 0).astype(jnp.bfloat16)
    width = own_ref.shape[1]
    work = []
    for side, weight_ref in enumerate((weight_own_ref, weight_other_ref)):
        columns = weight_ref.shape[2]
        queries = dot(feats[:half], weight_ref[0]).astype(jnp.bfloat16) * (HEAD_DIM ** -0.5)
        queries = queries.astype(jnp.bfloat16)
        keys = dot(feats[...], weight_ref[1]).astype(jnp.bfloat16)
        values = dot(feats[...], weight_ref[2]).astype(jnp.bfloat16)
        work.append((queries, keys, values))
    stacks = width // HEAD_DIM // STACK

    def place(stack):
        at = stack * STACK * HEAD_DIM
        return work[at // columns], at % columns // LANES * LANES, at % LANES // HEAD_DIM

    def score(stack):
        (queries, keys, _), at, lowest = place(stack)
        query = jnp.concatenate(
            [
                jnp.where(lane[:half] // HEAD_DIM == lowest + head, queries[:, at : at + LANES], 0.0)
                for head in range(STACK)
            ],
            axis=0,
        ).astype(jnp.bfloat16)
        query = jnp.concatenate([query, jnp.concatenate([first] * STACK, axis=0)], axis=1)
        return dot_last(query, jnp.concatenate([keys[:, at : at + LANES], dead_block[...]], axis=1))

    def weigh(stack, exponent):
        (_, _, values), at, _ = place(stack)
        return dot(
            exponent, jnp.concatenate([values[:, at : at + LANES], jnp.ones(dead_block.shape, jnp.bfloat16)], axis=1)
        )

    wide = lax.broadcasted_iota(jnp.int32, (half, 2 * LANES), 1)
    scores = score(0)
    total = pending = None
    for stack in range(stacks + 1):
        following = score(stack + 1) if stack + 1 < stacks else None
        if pending is not None:
            result = weigh(stack - 1, pending)
            _, at, lowest = place(stack - 1)
            for head in range(STACK):
                piece = result[head * half : (head + 1) * half]
                mine = wide // HEAD_DIM % group_heads == lowest + head
                total = piece if lowest + head == 0 else jnp.where(mine, piece, total)
            if lowest + STACK == group_heads:
                end = stack * STACK * HEAD_DIM
                out_ref[:, end - LANES : end] = (total[:, :LANES] / total[:, LANES:]).astype(jnp.bfloat16)
        if stack < stacks:
            exponent = jnp.exp(scores - jnp.max(scores, axis=1, keepdims=True))
            pending = exponent.astype(jnp.bfloat16)
        scores = following


def mix_kernel(
    counts_ref, returned_hbm, stream_hbm, *refs,
):
    weights, mixed_ref = refs[:6], refs[6]
    stream_ref, returned_ref = refs[7:9]
    out_own_ref, out_other_ref, up_own_ref, up_other_ref, down_ref, semaphores, hidden = refs[9:]
    size = up_own_ref.shape[1]
    copies = start_copies(
        (stream_hbm, returned_hbm, *weights),
        (
            stream_ref, returned_ref, out_own_ref, out_other_ref, up_own_ref, up_other_ref,
            down_ref.at[:size], down_ref.at[size:],
        ),
        semaphores,
    )
    half = returned_ref.shape[0]
    columns = out_own_ref.shape[0]
    rep = lax.axis_index("rep")
    live = counts_ref[0]
    base = rep * half
    row = lax.broadcasted_iota(jnp.int32, (half, half), 0)
    copies[0].wait()
    hot = (row == stream_ref[half + 1 : half + 2, :half].astype(jnp.int32)).astype(jnp.bfloat16)
    copies[1].wait()
    restored = dot(hot, returned_ref[...]).astype(jnp.bfloat16)
    copies[2].wait()
    copies[3].wait()
    mid = (
        stream_ref[:half]
        + dot(restored[:, :columns], out_own_ref[...])
        + dot(restored[:, columns:], out_other_ref[...])
    )
    mlp_in = normalize(mid, stream_ref[half : half + 1]).astype(jnp.bfloat16)
    chunk = min(size, 512)
    for side, up_ref in enumerate((up_own_ref, up_other_ref)):
        copies[4 + side].wait()
        for at in range(0, size, chunk):
            lifted = dot(mlp_in, up_ref[:, at : at + chunk])
            hidden[:, side * size + at : side * size + at + chunk] = gelu(lifted).astype(jnp.bfloat16)
    copies[6].wait()
    copies[7].wait()
    mixed = mid + dot(hidden[...], down_ref[...])
    row = lax.broadcasted_iota(jnp.int32, mixed.shape, 0) + base
    mixed_ref[...] = jnp.where(row < live, mixed, 0.0).astype(jnp.bfloat16)


def call(kernel, out_shape, ins, scratch, flops, transcendentals, limit):
    bytes_accessed = 4 * MIB
    return pl.pallas_call(
        kernel,
        out_shape=out_shape,
        in_specs=ins,
        out_specs=jax.tree.map(lambda _: VMEM, out_shape),
        scratch_shapes=scratch,
        compiler_params=pltpu.CompilerParams(vmem_limit_bytes=limit),
        cost_estimate=pl.CostEstimate(
            flops=flops, bytes_accessed=bytes_accessed, transcendentals=transcendentals
        ),
    )


def shards(
    points,
    counts,
    neighbours,
    order_send,
    cpe_taps,
    cpe_linear,
    cpe_gain,
    attn_gain,
    qkv_weight,
    out_weight,
    mlp_gain,
    up_weight,
    down_weight,
):
    rows, width = points.shape
    half = rows // 2
    taps = neighbours.shape[0]
    ring = ("seg", "ord")
    peers = lax.axis_size("seg") * lax.axis_size("ord")
    per_peer = rows // peers
    per_half = per_peer // 2
    live = counts[0]

    def swap(array):
        return lax.ppermute(array, "rep", [(0, 1), (1, 0)])

    up_hop = [(i, i + 1) for i in range(peers - 1)]
    down_hop = [(i + 1, i) for i in range(peers - 1)]
    after = lax.ppermute(points[:RIM], ring, down_hop)
    before = lax.ppermute(lax.dynamic_slice_in_dim(points, live - RIM, RIM, 0), ring, up_hop)
    linear_other = swap(cpe_linear)
    qkv_own = qkv_weight.transpose(1, 0, 2)
    qkv_other = swap(qkv_own)
    out_other = swap(out_weight)
    up_other = swap(up_weight)
    down_other = swap(down_weight)
    tapping = 2 * taps * half * width
    tap_rows = jnp.concatenate([cpe_taps.astype(jnp.float32), order_send.astype(jnp.float32)], axis=0)
    rep = lax.axis_index("rep")
    own_neighbours = lax.dynamic_slice_in_dim(neighbours, rep * half, half, 1)
    convolved = call(
        convolve_kernel,
        jax.ShapeDtypeStruct((half, width), jnp.float32),
        [VMEM] * 3,
        [pltpu.VMEM((half, taps), jnp.int32)],
        tapping * (half + RIM),
        0,
        12 * MIB,
    )(points, own_neighbours, tap_rows)
    stream, send = call(
        functools.partial(encode_kernel, per_half),
        [
            jax.ShapeDtypeStruct((half + TILE, width), jnp.float32),
            jax.ShapeDtypeStruct((half, width), jnp.bfloat16),
        ],
        [SMEM] + [VMEM] * 11,
        [
            pltpu.VMEM((half, width), jnp.float32),
            pltpu.VMEM((half, width), jnp.float32),
            pltpu.VMEM((half, taps), jnp.int32),
        ],
        tapping * RIM,
        half * 4,
        12 * MIB,
    )(
        counts, before, points, after, own_neighbours, tap_rows, convolved,
        cpe_linear, linear_other, cpe_gain.reshape(1, width), attn_gain.reshape(1, width),
        mlp_gain.reshape(1, width),
    )

    arrived = lax.all_to_all(
        send.reshape(peers, per_half, width), ring, split_axis=0, concat_axis=0, tiled=True
    ).reshape(half, width)
    arrived_other = swap(arrived)
    attended = call(
        attend_kernel,
        jax.ShapeDtypeStruct((half, width), jnp.bfloat16),
        [VMEM] * 4,
        [pltpu.VMEM((rows, width), jnp.bfloat16), pltpu.VMEM((rows, LANES), jnp.bfloat16)],
        2 * (width // HEAD_DIM) * half * rows * 512,
        (width // HEAD_DIM) * half * rows,
        32 * MIB,
    )(arrived, arrived_other, qkv_own, qkv_other)
    returned = lax.all_to_all(
        attended.reshape(peers, per_half, width), ring, split_axis=0, concat_axis=0, tiled=True
    ).reshape(half, width)
    hidden = 2 * up_weight.shape[1]
    weights = (out_weight, out_other, up_weight, up_other, down_weight, down_other)
    return call(
        mix_kernel,
        jax.ShapeDtypeStruct((half, width), jnp.bfloat16),
        [SMEM] + [HBM] * 8,
        [pltpu.VMEM(array.shape, array.dtype) for array in (stream, returned, *weights[:4])]
        + [
            pltpu.VMEM((hidden, width), down_weight.dtype),
            pltpu.SemaphoreType.DMA((8,)),
            pltpu.VMEM((half, hidden), jnp.bfloat16),
        ],
        2 * half * width * (width + half + 2 * hidden),
        half * hidden,
        52 * MIB,
    )(counts, returned, stream, *weights)


def solution(mesh):
    placed = (
        P(("tile", "seg", "ord"), None),
        P(("tile", "seg", "ord")),
        P(None, ("tile", "seg", "ord")),
        P(("tile", "seg", "ord"), None),
        P(),
        P(None, "rep"),
        P(),
        P(),
        P(None, None, "rep"),
        P("rep", None),
        P(),
        P(None, "rep"),
        P("rep", None),
    )
    return jax.shard_map(
        shards,
        mesh=mesh,
        in_specs=placed,
        out_specs=P(("tile", "seg", "ord", "rep"), None),
        check_vma=False,
    )
```

```python
import functools

import jax
import jax.numpy as jnp
from jax import lax
from jax.experimental import pallas as pl
from jax.experimental.pallas import tpu as pltpu
from jax.sharding import PartitionSpec as P

RIM = 128
HEAD_DIM = 16
LANES = 128
TILE = 8
STACK = 2
EPSILON = 1e-06
MASKED = -1e30
DEAD_MARK = 16384.0
DEAD_LEVEL = 8192.0

VMEM = pl.BlockSpec(memory_space=pltpu.VMEM)
SMEM = pl.BlockSpec(memory_space=pltpu.SMEM)
HBM = pl.BlockSpec(memory_space=pltpu.HBM)
MIB = 1 << 20


def dot(a, b):
    return jnp.dot(a, b, preferred_element_type=jnp.float32)


def dot_first(a, b):
    return lax.dot_general(a, b, (((0,), (0,)), ((), ())), preferred_element_type=jnp.float32)


def dot_last(a, b):
    return lax.dot_general(a, b, (((1,), (1,)), ((), ())), preferred_element_type=jnp.float32)


def normalize(values, gain):
    centred = values - jnp.mean(values, axis=-1, keepdims=True)
    spread = jnp.mean(centred * centred, axis=-1, keepdims=True)
    return centred * lax.rsqrt(spread + EPSILON) * gain


def gelu(x):
    return 0.5 * x * (1.0 + jnp.tanh((2.0 / jnp.pi) ** 0.5 * (x + 0.044715 * (x * x * x))))


def own_order(order, base, rep, half, per_half):
    slots = order.shape[1]
    local = jnp.clip(order - base, 0, half - 1).astype(jnp.float32)
    local = jnp.broadcast_to(local, (16, slots)).astype(jnp.bfloat16)
    spot = lax.broadcasted_iota(jnp.int32, (1, half), 1)
    source = (spot // per_half) * (2 * per_half) + rep * per_half + spot % per_half
    hot = (lax.broadcasted_iota(jnp.int32, (slots, half), 0) == source).astype(jnp.bfloat16)
    return dot(local, hot)[:1].astype(jnp.int32)


def add_taps(acc_ref, at, rows, index_ref, offset, source, taps_ref):
    index = index_ref[pl.ds(at, rows)] - offset
    spots = lax.broadcasted_iota(jnp.int32, (rows, source.shape[0]), 1)
    for tap in range(1, index_ref.shape[1]):
        hot = (spots == index[:, tap : tap + 1]).astype(jnp.bfloat16)
        acc_ref[pl.ds(at, rows)] += dot(hot, source) * taps_ref[tap : tap + 1, :]


def convolve_kernel(points_ref, neighbours_ref, taps_ref, acc_ref, index_ref):
    half = acc_ref.shape[0]
    rep = lax.axis_index("rep")
    base = pl.multiple_of(rep * half, half)
    index_ref[...] = neighbours_ref[...].T
    acc_ref[...] = points_ref[pl.ds(base, half)].astype(jnp.float32) * taps_ref[:1]
    edge = pl.multiple_of(rep * RIM, RIM)
    add_taps(acc_ref, edge, RIM, index_ref, RIM + base, points_ref[pl.ds(base, half)], taps_ref)
    inner = pl.multiple_of((1 - rep) * RIM, RIM)
    start = pl.multiple_of(rep * RIM, RIM)
    span = half + RIM
    add_taps(acc_ref, inner, RIM, index_ref, RIM + start, points_ref[pl.ds(start, span)], taps_ref)


def encode_kernel(
    per_half, counts_ref, before_ref, points_ref, after_ref, neighbours_ref, taps_ref,
    own_ref, linear_own_ref, linear_other_ref, cpe_gain_ref, attn_gain_ref,
    stream_ref, send_ref,
    acc, encoded, index_ref,
):
    rows, half = points_ref.shape[0], send_ref.shape[0]
    rep = lax.axis_index("rep")
    live = counts_ref[0]
    base = pl.multiple_of(rep * half, half)
    acc[...] = own_ref[...]
    index_ref[...] = neighbours_ref[...].T

    @pl.when(rep == 0)
    def _():
        add_taps(acc, 0, RIM, index_ref, 0, before_ref[...], taps_ref)

    reach = live - RIM - base

    @pl.when((reach > -RIM) & (reach < half))
    def _():
        span = RIM + TILE
        at = pl.multiple_of(jnp.clip(reach // TILE * TILE, 0, half - span), TILE)
        add_taps(acc, at, span, index_ref, RIM + rows, after_ref[...], taps_ref)

    convolved = acc[...].astype(jnp.bfloat16)
    columns = linear_own_ref.shape[1]
    own_at = pl.multiple_of(rep * columns, columns)
    other_at = pl.multiple_of((1 - rep) * columns, columns)
    encoded[:, pl.ds(own_at, columns)] = dot(convolved, linear_own_ref[...])
    encoded[:, pl.ds(other_at, columns)] = dot(convolved, linear_other_ref[...])
    rounded = encoded[...].astype(jnp.bfloat16).astype(jnp.float32)
    own_points = points_ref[pl.ds(base, half)].astype(jnp.float32)
    stream = own_points + normalize(rounded, cpe_gain_ref[...])
    stream_ref[:half] = stream
    normed = normalize(stream, attn_gain_ref[...])
    row = lax.broadcasted_iota(jnp.int32, normed.shape, 0) + base
    marked = jnp.where(row < live, normed, DEAD_MARK).astype(jnp.bfloat16)
    source = lax.broadcasted_iota(jnp.int32, (half, half), 0) + base
    taps = neighbours_ref.shape[0]
    order = own_order(taps_ref[taps : taps + 1].astype(jnp.int32), base, rep, half, per_half)
    hot = (source - base == order).astype(jnp.bfloat16)
    send_ref[...] = dot_first(hot, marked).astype(jnp.bfloat16)
    stream_ref[half : half + 1, :half] = order.astype(jnp.float32)


def start_copies(sources, targets, semaphores):
    copies = [
        pltpu.make_async_copy(source, target, semaphores.at[at])
        for at, (source, target) in enumerate(zip(sources, targets))
    ]
    for copy in copies:
        copy.start()
    return copies


def attend_kernel(
    own_ref, other_ref, weight_own_ref, weight_other_ref, gain_ref, out_ref, gain_out_ref,
    feats, dead_block,
):
    gain_out_ref[...] = jnp.broadcast_to(gain_ref[...], gain_out_ref.shape)
    half = own_ref.shape[0]
    group_heads = LANES // HEAD_DIM
    lane = lax.broadcasted_iota(jnp.int32, (2 * half, LANES), 1)
    for at, ref in ((0, own_ref), (half, other_ref)):
        rows = ref[...].astype(jnp.float32)
        dead = rows > DEAD_LEVEL
        feats[at : at + half] = jnp.where(dead, 0.0, rows).astype(jnp.bfloat16)
        dead_block[at : at + half] = jnp.where(
            dead[:, :LANES] & (lane[:half] == 0), MASKED, 0.0
        ).astype(jnp.bfloat16)
    first = (lane[:half] == 0).astype(jnp.bfloat16)
    width = own_ref.shape[1]
    work = []
    for side, weight_ref in enumerate((weight_own_ref, weight_other_ref)):
        columns = weight_ref.shape[2]
        queries = dot(feats[:half], weight_ref[0]).astype(jnp.bfloat16) * (HEAD_DIM ** -0.5)
        queries = queries.astype(jnp.bfloat16)
        keys = dot(feats[...], weight_ref[1]).astype(jnp.bfloat16)
        values = dot(feats[...], weight_ref[2]).astype(jnp.bfloat16)
        work.append((queries, keys, values))
    stacks = width // HEAD_DIM // STACK

    def place(stack):
        at = stack * STACK * HEAD_DIM
        return work[at // columns], at % columns // LANES * LANES, at % LANES // HEAD_DIM

    def score(stack):
        (queries, keys, _), at, lowest = place(stack)
        query = jnp.concatenate(
            [
                jnp.where(lane[:half] // HEAD_DIM == lowest + head, queries[:, at : at + LANES], 0.0)
                for head in range(STACK)
            ],
            axis=0,
        ).astype(jnp.bfloat16)
        query = jnp.concatenate([query, jnp.concatenate([first] * STACK, axis=0)], axis=1)
        return dot_last(query, jnp.concatenate([keys[:, at : at + LANES], dead_block[...]], axis=1))

    def weigh(stack, exponent):
        (_, _, values), at, _ = place(stack)
        return dot(
            exponent, jnp.concatenate([values[:, at : at + LANES], jnp.ones(dead_block.shape, jnp.bfloat16)], axis=1)
        )

    wide = lax.broadcasted_iota(jnp.int32, (half, 2 * LANES), 1)
    scores = score(0)
    total = pending = None
    for stack in range(stacks + 1):
        following = score(stack + 1) if stack + 1 < stacks else None
        if pending is not None:
            result = weigh(stack - 1, pending)
            _, at, lowest = place(stack - 1)
            for head in range(STACK):
                piece = result[head * half : (head + 1) * half]
                mine = wide // HEAD_DIM % group_heads == lowest + head
                total = piece if lowest + head == 0 else jnp.where(mine, piece, total)
            if lowest + STACK == group_heads:
                end = stack * STACK * HEAD_DIM
                out_ref[:, end - LANES : end] = (total[:, :LANES] / total[:, LANES:]).astype(jnp.bfloat16)
        if stack < stacks:
            exponent = jnp.exp(scores - jnp.max(scores, axis=1, keepdims=True))
            pending = exponent.astype(jnp.bfloat16)
        scores = following


def mix_kernel(
    counts_ref, returned_hbm, stream_hbm, gain_hbm, *refs,
):
    weights, mixed_ref = refs[:6], refs[6]
    stream_ref, returned_ref, gain_ref = refs[7:10]
    out_ref, up_own_ref, up_other_ref, down_ref, semaphores, hidden = refs[10:]
    columns = out_ref.shape[0] // 2
    size = up_own_ref.shape[1]
    copies = start_copies(
        (stream_hbm, returned_hbm, gain_hbm, *weights),
        (
            stream_ref, returned_ref, gain_ref, out_ref.at[:columns], out_ref.at[columns:],
            up_own_ref, up_other_ref,
            down_ref.at[:size], down_ref.at[size:],
        ),
        semaphores,
    )
    half = returned_ref.shape[0]
    rep = lax.axis_index("rep")
    live = counts_ref[0]
    base = rep * half
    row = lax.broadcasted_iota(jnp.int32, (half, half), 0)
    copies[0].wait()
    hot = (row == stream_ref[half : half + 1, :half].astype(jnp.int32)).astype(jnp.bfloat16)
    copies[1].wait()
    restored = dot(hot, returned_ref[...]).astype(jnp.bfloat16)
    for copy in copies[2:5]:
        copy.wait()
    mid = stream_ref[:half] + dot(restored, out_ref[...])
    mlp_in = normalize(mid, gain_ref[:1]).astype(jnp.bfloat16)
    chunk = min(size, 512)
    for side, up_ref in enumerate((up_own_ref, up_other_ref)):
        copies[5 + side].wait()
        for at in range(0, size, chunk):
            lifted = dot(mlp_in, up_ref[:, at : at + chunk])
            hidden[:, side * size + at : side * size + at + chunk] = gelu(lifted).astype(jnp.bfloat16)
    copies[7].wait()
    copies[8].wait()
    mixed = mid + dot(hidden[...], down_ref[...])
    row = lax.broadcasted_iota(jnp.int32, mixed.shape, 0) + base
    mixed_ref[...] = jnp.where(row < live, mixed, 0.0).astype(jnp.bfloat16)


def call(kernel, out_shape, ins, scratch, flops, transcendentals, limit):
    bytes_accessed = 4 * MIB
    return pl.pallas_call(
        kernel,
        out_shape=out_shape,
        in_specs=ins,
        out_specs=jax.tree.map(lambda _: VMEM, out_shape),
        scratch_shapes=scratch,
        compiler_params=pltpu.CompilerParams(vmem_limit_bytes=limit),
        cost_estimate=pl.CostEstimate(
            flops=flops, bytes_accessed=bytes_accessed, transcendentals=transcendentals
        ),
    )


def shards(
    points,
    counts,
    neighbours,
    order_send,
    cpe_taps,
    cpe_linear,
    cpe_gain,
    attn_gain,
    qkv_weight,
    out_weight,
    mlp_gain,
    up_weight,
    down_weight,
):
    rows, width = points.shape
    half = rows // 2
    taps = neighbours.shape[0]
    ring = ("seg", "ord")
    peers = lax.axis_size("seg") * lax.axis_size("ord")
    per_peer = rows // peers
    per_half = per_peer // 2
    live = counts[0]

    def swap(array):
        return lax.ppermute(array, "rep", [(0, 1), (1, 0)])

    up_hop = [(i, i + 1) for i in range(peers - 1)]
    down_hop = [(i + 1, i) for i in range(peers - 1)]
    after = lax.ppermute(points[:RIM], ring, down_hop)
    before = lax.ppermute(lax.dynamic_slice_in_dim(points, live - RIM, RIM, 0), ring, up_hop)
    linear_other = swap(cpe_linear)
    qkv_own = qkv_weight.transpose(1, 0, 2)
    qkv_other = swap(qkv_own)
    out_other = swap(out_weight)
    up_other = swap(up_weight)
    down_other = swap(down_weight)
    tapping = 2 * taps * half * width
    tap_rows = jnp.concatenate([cpe_taps.astype(jnp.float32), order_send.astype(jnp.float32)], axis=0)
    rep = lax.axis_index("rep")
    own_neighbours = lax.dynamic_slice_in_dim(neighbours, rep * half, half, 1)
    convolved = call(
        convolve_kernel,
        jax.ShapeDtypeStruct((half, width), jnp.float32),
        [VMEM] * 3,
        [pltpu.VMEM((half, taps), jnp.int32)],
        tapping * (half + RIM),
        0,
        12 * MIB,
    )(points, own_neighbours, tap_rows)
    stream, send = call(
        functools.partial(encode_kernel, per_half),
        [
            jax.ShapeDtypeStruct((half + TILE, width), jnp.float32),
            jax.ShapeDtypeStruct((half, width), jnp.bfloat16),
        ],
        [SMEM] + [VMEM] * 10,
        [
            pltpu.VMEM((half, width), jnp.float32),
            pltpu.VMEM((half, width), jnp.float32),
            pltpu.VMEM((half, taps), jnp.int32),
        ],
        tapping * RIM,
        half * 4,
        12 * MIB,
    )(
        counts, before, points, after, own_neighbours, tap_rows, convolved,
        cpe_linear, linear_other, cpe_gain.reshape(1, width), attn_gain.reshape(1, width),
    )

    arrived = lax.all_to_all(
        send.reshape(peers, per_half, width), ring, split_axis=0, concat_axis=0, tiled=True
    ).reshape(half, width)
    arrived_other = swap(arrived)
    attended, gain = call(
        attend_kernel,
        [
            jax.ShapeDtypeStruct((half, width), jnp.bfloat16),
            jax.ShapeDtypeStruct((TILE, width), jnp.float32),
        ],
        [VMEM] * 5,
        [pltpu.VMEM((rows, width), jnp.bfloat16), pltpu.VMEM((rows, LANES), jnp.bfloat16)],
        2 * (width // HEAD_DIM) * half * rows * 512,
        (width // HEAD_DIM) * half * rows,
        32 * MIB,
    )(arrived, arrived_other, qkv_own, qkv_other, mlp_gain.reshape(1, width))
    returned = lax.all_to_all(
        attended.reshape(peers, per_half, width), ring, split_axis=0, concat_axis=0, tiled=True
    ).reshape(half, width)
    hidden = 2 * up_weight.shape[1]
    weights = (out_weight, out_other, up_weight, up_other, down_weight, down_other)
    return call(
        mix_kernel,
        jax.ShapeDtypeStruct((half, width), jnp.bfloat16),
        [SMEM] + [HBM] * 9,
        [pltpu.VMEM(array.shape, array.dtype) for array in (stream, returned, gain)]
        + [
            pltpu.VMEM((width, width), out_weight.dtype),
            pltpu.VMEM(up_weight.shape, up_weight.dtype),
            pltpu.VMEM(up_weight.shape, up_weight.dtype),
            pltpu.VMEM((hidden, width), down_weight.dtype),
            pltpu.SemaphoreType.DMA((9,)),
            pltpu.VMEM((half, hidden), jnp.bfloat16),
        ],
        2 * half * width * (width + half + 2 * hidden),
        half * hidden,
        52 * MIB,
    )(counts, returned, stream, gain, *weights)


def solution(mesh):
    placed = (
        P(("tile", "seg", "ord"), None),
        P(("tile", "seg", "ord")),
        P(None, ("tile", "seg", "ord")),
        P(("tile", "seg", "ord"), None),
        P(),
        P(None, "rep"),
        P(),
        P(),
        P(None, None, "rep"),
        P("rep", None),
        P(),
        P(None, "rep"),
        P("rep", None),
    )
    return jax.shard_map(
        shards,
        mesh=mesh,
        in_specs=placed,
        out_specs=P(("tile", "seg", "ord", "rep"), None),
        check_vma=False,
    )
```
